32 devices in a mesh: docs: 8 (over y, x, core), rep: 4 (over z).
Axes of the slice: x: 2, y: 2, z: 4, core: 2. Of those that a mesh axis runs over, the one named last changes fastest.
Arguments:
- embeds: bfloat16 [8192, 1024], P(('docs', 'rep'))
- cluster: int32 [8192], P(('docs', 'rep')), may hold values from 0 to 15, as said below
Outputs:
- top_sim: float32 [8192], P(('docs', 'rep'))
- dup_mass: float32 [8192], P(('docs', 'rep'))
The draws below stay inside these ranges and needn't reach their ends.
Inputs may be any that keep to these rules, and one draw needn't show every extreme that they name: Cluster ids never fall along the documents and every id is used; each cluster has at most 3074 documents, and some cluster has exactly that many and meets five consecutive blocks of 1024 documents; no cluster meets more than five.
All inputs are finite; a program needn't handle non-finite values.
Results may differ from the reference program's by a relative error of at most 0.00057.
Values may be sent and summed in bfloat16 or wider, within the bound.
A program may use at most 64 MiB of HBM per device.

```python
import jax
import jax.numpy as jnp
from jax import lax

D = 1024
QDOC = 256
DOCS = 8192
NCLUST = 16
N_DOCS = 8
N_REP = 4


def widest_block(key):
    key = jax.random.fold_in(key, 977)
    keys = jax.random.split(key, 2)
    group = jax.random.randint(keys[0], (), 0, N_DOCS // 8).astype(jnp.int32)
    offset = jax.random.randint(keys[1], (), 0, 3).astype(jnp.int32)
    return (group * 8 + offset).astype(jnp.int32)


def draw_cluster(key, part):
    first_block = widest_block(key)
    key = jax.random.fold_in(key, 2)
    keys = jax.random.split(key, 3)
    block = QDOC * N_REP
    span = 8 * block
    groups = N_DOCS // 8
    group_ids = jnp.arange(groups, dtype=jnp.int32)
    widest_group = first_block // 8
    lengths = jax.random.randint(keys[0], (groups,), 2 * block + 1, 3 * block + 3).astype(jnp.int32)
    lengths = jnp.where(group_ids == widest_group, 3 * block + 2, lengths)
    room = span - lengths
    offsets = jax.random.randint(keys[1], (groups,), 0, 2 ** 20).astype(jnp.int32) % (room - 1) + 1
    widest_offset = (first_block - widest_group * 8 + 1) * block - 1
    offsets = jnp.where(group_ids == widest_group, widest_offset, offsets)
    big_starts = group_ids * span + offsets
    big_ends = big_starts + lengths
    position = jnp.arange(DOCS, dtype=jnp.int32)
    group_of = position // span
    start_here = big_starts[group_of]
    end_here = big_ends[group_of]
    inside = (position > start_here) & (position < end_here)
    grid = (position % (2 * block) == 0) & jnp.logical_not(inside)
    forced = grid | (position == start_here) | (position == end_here)
    eligible = jnp.logical_not(forced) & jnp.logical_not(inside)
    picks = NCLUST - jnp.sum(forced.astype(jnp.int32))
    spread = 2 ** 30 // DOCS
    scores = jax.random.randint(keys[2], (DOCS,), 0, spread).astype(jnp.int32) * DOCS + position
    scores = jnp.where(eligible, scores, -1)
    ordered = jnp.sort(scores)[::-1]
    threshold = ordered[picks - 1]
    chosen = eligible & (scores >= threshold)
    starts = (forced | chosen).astype(jnp.int32)
    return (jnp.cumsum(starts) - 1).astype(jnp.int32)


def draw_embeds(key, part):
    first_block = widest_block(key)
    key = jax.random.fold_in(key, 1)
    keys = jax.random.split(key, 6)
    base = jax.random.normal(keys[0], (DOCS, D), jnp.float32)
    scales = jax.random.uniform(keys[1], (DOCS, 1), jnp.float32, 0.5, 2.0)
    first_off = jax.random.randint(keys[2], (), 1, QDOC * N_REP)
    second_off = jax.random.randint(keys[3], (), QDOC * N_REP, 3 * QDOC * N_REP)
    first_mix = jax.random.uniform(keys[4], (DOCS, 1), jnp.float32, 0.0, 1.5)
    second_mix = jax.random.uniform(keys[5], (DOCS, 1), jnp.float32, 0.0, 1.5)
    mixed = base + first_mix * jnp.roll(base, first_off, axis=0) + second_mix * jnp.roll(base, second_off, axis=0)
    block = QDOC * N_REP
    first_row = first_block * block + block - 1
    last_row = first_row + 3 * block + 1
    source_row = lax.dynamic_slice_in_dim(mixed, first_row, 1, 0)
    noise_row = lax.dynamic_slice_in_dim(base, last_row, 1, 0)
    row_index = jnp.arange(DOCS, dtype=jnp.int32)[:, None]
    mixed = jnp.where(row_index == last_row, source_row + 0.15 * noise_row, mixed)
    return (mixed * scales).astype(jnp.bfloat16)


def setup_inputs(seed: int = 0) -> dict:
    seeds = jax.random.split(jax.random.key(seed), 3)
    return {
        "embeds": draw_embeds(jax.random.fold_in(seeds[2], 71), 0),
        "cluster": draw_cluster(jax.random.fold_in(seeds[2], 71), 0),
    }


dup_scale = 8.0

def reference(embeds, cluster):
    x = embeds.astype(jnp.float32)
    unit = (x * lax.rsqrt(lax.optimization_barrier(jnp.mean(x * x, axis=1, keepdims=True)) + 1e-06) * D ** (-0.5)).astype(jnp.bfloat16)
    block = QDOC * N_REP
    reach = 4
    pad_unit = jnp.pad(unit, ((reach * block, reach * block), (0, 0)))
    pad_ids = jnp.pad(cluster, (reach * block, reach * block), constant_values=-1)
    position = jnp.arange(DOCS, dtype=jnp.int32)
    pad_pos = jnp.pad(position, (reach * block, reach * block), constant_values=-1)
    width = (2 * reach + 1) * block

    def one_block(index):
        start = (index * block).astype(jnp.int32)
        rows = lax.dynamic_slice_in_dim(unit, start, block, 0)
        row_ids = lax.dynamic_slice_in_dim(cluster, start, block, 0)
        row_pos = lax.dynamic_slice_in_dim(position, start, block, 0)
        window = lax.dynamic_slice_in_dim(pad_unit, start, width, 0)
        win_ids = lax.dynamic_slice_in_dim(pad_ids, start, width, 0)
        win_pos = lax.dynamic_slice_in_dim(pad_pos, start, width, 0)
        scores = lax.dot_general(rows, window, (((1,), (1,)), ((), ())), preferred_element_type=jnp.float32)
        mask = (row_ids[:, None] == win_ids[None, :]) & (row_pos[:, None] != win_pos[None, :])
        top = lax.optimization_barrier(jnp.max(jnp.where(mask, scores, -1.0), axis=1))
        mass = lax.optimization_barrier(jnp.sum(jnp.where(mask, jnp.exp(dup_scale * (scores - 1.0)), 0.0), axis=1))
        return (top, mass)
    top, mass = lax.map(one_block, jnp.arange(N_DOCS, dtype=jnp.int32))
    return (top.reshape(-1), mass.reshape(-1))
```

```python
import functools
import math

import jax
import jax.numpy as jnp
from jax import lax
from jax.experimental import pallas as pl
from jax.experimental.pallas import tpu as pltpu
from jax.sharding import PartitionSpec as P

MESH = pl.DeviceIdType.MESH
dup_scale = 8.0
LOG2 = dup_scale * math.log2(math.e)
NO_PAIR = -100.0
REACH = 3
SLOTS = 2 * REACH + 1
OWN, ZA, ZB = REACH, SLOTS, SLOTS + 1


def kernel(
    n, e_ref, c_ref, top_ref, mass_ref, buf, corner, xids, racc, cacc, rowres, rbuf, ssem, rsem
):
    q, width = e_ref.shape
    d = lax.axis_index("docs")
    z = lax.axis_index("rep")
    odd = lax.rem(d, 2)
    sister = d + 1 - 2 * odd
    to_a = jnp.where(z < 2, z + 2, 3 - z)
    from_a = jnp.where(z < 2, 3 - z, z - 2)
    mate = z + 1 - 2 * lax.rem(z, 2)
    inner = (z == 1) | (z == 2)
    outer = (z == 0) | (z == 3)

    def has(k):
        return (d + k >= 0) & (d + k < n)

    corner_in = (z == 0) & has(-4)
    corner_out = (z == 3) & has(4)

    def remote(src, dst, s, r, dev):
        return pltpu.make_async_remote_copy(
            src_ref=src,
            dst_ref=dst,
            send_sem=ssem.at[s],
            recv_sem=rsem.at[r],
            device_id=dev,
            device_id_type=MESH,
        )

    barrier = pltpu.get_barrier_semaphore()

    def greet(dev):
        pl.semaphore_signal(barrier, inc=1, device_id=dev, device_id_type=MESH)

    total = jnp.int32(3)
    for k in (-3, -2, -1, 1, 2, 3):
        pl.when(has(k))(functools.partial(greet, (d + k, z)))
        total = total + has(k).astype(jnp.int32)
    greet((d, to_a))
    greet((d, from_a))
    greet((d, mate))
    pl.when(corner_in)(functools.partial(greet, (d - 4, 3)))
    pl.when(corner_out)(functools.partial(greet, (d + 4, 0)))
    total = total + corner_in.astype(jnp.int32) + corner_out.astype(jnp.int32)

    x = e_ref[...].astype(jnp.float32)
    scale = lax.rsqrt(jnp.mean(x * x, axis=1, keepdims=True) + 1e-06)
    buf[OWN, 0:q, :] = (x * scale * width ** (-0.5)).astype(jnp.bfloat16)
    ids = c_ref[...].astype(jnp.float32)
    buf[OWN, q : q + 16, :] = jnp.zeros((16, width), jnp.bfloat16)
    buf[OWN, q : q + 16, 0:q] = jnp.broadcast_to(ids, (16, q)).astype(jnp.bfloat16)

    pl.semaphore_wait(barrier, total)

    own = buf.at[OWN]
    send_a = remote(own, buf.at[ZA], 6, ZA, (d, to_a))
    send_b = remote(own, buf.at[ZB], 7, ZB, (d, mate))
    send_p2 = remote(own, buf.at[REACH - 2], 1, REACH - 2, (d + 2, z))
    send_m2 = remote(own, buf.at[REACH + 2], 2, REACH + 2, (d - 2, z))
    sis_slot = REACH - 1 + 2 * odd
    send_sis = remote(own, buf.at[sis_slot], 0, sis_slot, (sister, z))
    far = 6 * odd - 3
    far_slot = REACH - far
    send_far = remote(own, buf.at[far_slot], 3, far_slot, (d + far, z))
    has_far = has(far)
    tail = pl.ds(q - 16, 32)
    send_corner = remote(buf.at[OWN, tail], corner, 8, SLOTS + 2, (d + 4, 0))

    pl.when(has(2))(send_p2.start)
    pl.when(has(-2))(send_m2.start)
    send_a.start()
    pl.when(outer)(send_b.start)
    send_sis.start()
    pl.when(has_far)(send_far.start)
    pl.when(corner_out)(send_corner.start)

    lanes = lax.broadcasted_iota(jnp.int32, (8, q), 1)
    subs = lax.broadcasted_iota(jnp.int32, (8, q), 0)

    def take_ids(slot):
        return buf[slot, q : q + 16, 0:q].astype(jnp.float32)[0:1]

    def load_x(slot, xi):
        row = jnp.broadcast_to(take_ids(slot), (128, q))
        xids[xi] = row.T
        racc[xi, 0] = jnp.full((q, 128), -1.0, jnp.float32)
        racc[xi, 1] = jnp.zeros((q, 128), jnp.float32)

    def tile(xslot, xi, slot, diagonal=False):
        scores = lax.dot_general(
            buf[xslot, 0:q, :],
            buf[slot, 0:q, :],
            (((1,), (1,)), ((), ())),
            preferred_element_type=jnp.float32,
        )
        yid = take_ids(slot)
        xid = xids[xi]
        tops, masses = [], []
        for lo in range(0, q, 128):
            mask = xid == yid[:, lo : lo + 128]
            if diagonal:
                i = lax.broadcasted_iota(jnp.int32, (q, 128), 0)
                j = lax.broadcasted_iota(jnp.int32, (q, 128), 1) + lo
                mask = mask & (i != j)
            top = jnp.where(mask, scores[:, lo : lo + 128], NO_PAIR)
            mass = jnp.exp2(top * LOG2 - LOG2)
            cols = pl.ds(lo, 128)
            cacc[slot, 0, :, cols] = jnp.maximum(
                cacc[slot, 0, :, cols], jnp.max(top.reshape(q // 8, 8, 128), axis=0)
            )
            cacc[slot, 1, :, cols] += jnp.sum(mass.reshape(q // 8, 8, 128), axis=0)
            tops.append(top)
            masses.append(mass)
        if not diagonal:
            racc[xi, 0] = jnp.maximum(racc[xi, 0], functools.reduce(jnp.maximum, tops))
            racc[xi, 1] += functools.reduce(jnp.add, masses)

    def row_result(xi):
        top = jnp.max(racc[xi, 0].T.reshape(16, 8, q), axis=0)
        mass = jnp.sum(racc[xi, 1].T.reshape(16, 8, q), axis=0)
        return top, mass

    cacc[:, 0] = jnp.full((SLOTS, 8, q), -1.0, jnp.float32)
    cacc[:, 1] = jnp.zeros((SLOTS, 8, q), jnp.float32)

    load_x(OWN, 0)
    tile(OWN, 0, OWN, diagonal=True)

    def arrived(slot):
        remote(own, buf.at[slot], 0, slot, (sister, z)).wait_recv()

    fwd_p2 = remote(
        buf.at[REACH + 2], buf.at[REACH + 1 + 2 * odd], 4, REACH + 1 + 2 * odd, (sister, z)
    )
    fwd_m2 = remote(
        buf.at[REACH - 2], buf.at[REACH - 3 + 2 * odd], 5, REACH - 3 + 2 * odd, (sister, z)
    )

    @pl.when(has(2))
    def _():
        arrived(REACH + 2)
        fwd_p2.start()

    @pl.when(has(-2))
    def _():
        arrived(REACH - 2)
        fwd_m2.start()

    for k in (1, -1, 3, -3):
        pl.when(has(k))(functools.partial(arrived, REACH + k))

    def own_step(slot, carry):
        @pl.when(has(slot - REACH))
        def _():
            tile(OWN, 0, slot)

        return carry

    lax.fori_loop(OWN + 1, SLOTS, own_step, 0)

    def other_quarter(xslot, xi, s, r, dev):
        arrived(xslot)
        load_x(xslot, xi)

        def step(slot, carry):
            @pl.when(has(slot - REACH))
            def _():
                tile(xslot, xi, slot)

            return carry

        lax.fori_loop(0, SLOTS, step, 0)
        top, mass = row_result(xi)
        rowres[xi - 1, 0] = top
        rowres[xi - 1, 1] = mass
        remote(rowres.at[xi - 1], rbuf.at[r], s, SLOTS + 3 + r, dev).start()

    @pl.when(inner)
    def _():
        other_quarter(ZB, 2, 17, ZB, (d, mate))

    other_quarter(ZA, 1, 16, ZA, (d, from_a))

    back = remote(rowres.at[2], rbuf.at[SLOTS + 2], 18, 2 * SLOTS + 5, (d - 4, 3))

    @pl.when(corner_in)
    def _():
        remote(buf.at[OWN, tail], corner, 8, SLOTS + 2, (d - 4, 3)).wait_recv()
        first = buf[OWN, 0:16, :].astype(jnp.float32)[0:1]
        last = corner[0:16, :].astype(jnp.float32)[15:16]
        cos = jnp.sum(first * last, axis=1, keepdims=True)
        here = take_ids(OWN)[:, 0:1]
        there = corner[16:32, 0:q].astype(jnp.float32)[0:1, q - 1 : q]
        top = jnp.broadcast_to(jnp.where(here == there, cos, NO_PAIR), (8, q))
        mass = jnp.exp2(top * LOG2 - LOG2)
        mine = (lanes == 0) & (subs == 0)
        cacc[OWN, 0] = jnp.maximum(cacc[OWN, 0], jnp.where(mine, top, -1.0))
        cacc[OWN, 1] += jnp.where(mine, mass, 0.0)
        theirs = (lanes == q - 1) & (subs == 0)
        rowres[2, 0] = jnp.where(theirs, top, -1.0)
        rowres[2, 1] = jnp.where(theirs, mass, 0.0)
        back.start()

    def result(k):
        return remote(
            cacc.at[REACH + k],
            rbuf.at[REACH - k],
            9 + REACH + k,
            SLOTS + 3 + REACH - k,
            (d + k, z),
        )

    for k in (-3, -2, -1, 1, 2, 3):
        pl.when(has(k))(result(k).start)

    top, mass = row_result(0)
    top_ref[...] = jnp.max(jnp.maximum(top, cacc[OWN, 0]), axis=0, keepdims=True)
    mass_ref[...] = jnp.sum(mass + cacc[OWN, 1], axis=0, keepdims=True)

    def add_result(slot):
        remote(rowres.at[0], rbuf.at[slot], 16, SLOTS + 3 + slot, (sister, z)).wait_recv()
        top_ref[...] = jnp.maximum(
            top_ref[...], jnp.max(rbuf[slot, 0], axis=0, keepdims=True)
        )
        mass_ref[...] += jnp.sum(rbuf[slot, 1], axis=0, keepdims=True)

    pl.when(corner_out)(functools.partial(add_result, SLOTS + 2))
    for k in (-3, -2, -1, 1, 2, 3):
        pl.when(has(k))(functools.partial(add_result, REACH + k))
    add_result(ZA)
    pl.when(outer)(functools.partial(add_result, ZB))

    pl.when(has(2))(send_p2.wait_send)
    pl.when(has(-2))(send_m2.wait_send)
    send_a.wait_send()
    pl.when(outer)(send_b.wait_send)
    send_sis.wait_send()
    pl.when(has_far)(send_far.wait_send)
    pl.when(corner_out)(send_corner.wait_send)
    pl.when(has(2))(fwd_p2.wait_send)
    pl.when(has(-2))(fwd_m2.wait_send)
    for k in (-3, -2, -1, 1, 2, 3):
        pl.when(has(k))(result(k).wait_send)
    remote(rowres.at[0], rbuf.at[ZA], 16, SLOTS + 3 + ZA, (d, from_a)).wait_send()

    @pl.when(inner)
    def _():
        remote(rowres.at[1], rbuf.at[ZB], 17, SLOTS + 3 + ZB, (d, mate)).wait_send()

    pl.when(corner_in)(back.wait_send)


def per_device(n, embeds, cluster):
    q, width = embeds.shape
    top, mass = pl.pallas_call(
        functools.partial(kernel, n),
        out_shape=(jax.ShapeDtypeStruct((1, q), jnp.float32),) * 2,
        in_specs=[pl.BlockSpec(memory_space=pltpu.VMEM)] * 2,
        out_specs=(pl.BlockSpec(memory_space=pltpu.VMEM),) * 2,
        scratch_shapes=[
            pltpu.VMEM((SLOTS + 2, q + 16, width), jnp.bfloat16),
            pltpu.VMEM((32, width), jnp.bfloat16),
            pltpu.VMEM((3, q, 128), jnp.float32),
            pltpu.VMEM((3, 2, q, 128), jnp.float32),
            pltpu.VMEM((SLOTS, 2, 8, q), jnp.float32),
            pltpu.VMEM((3, 2, 8, q), jnp.float32),
            pltpu.VMEM((SLOTS + 3, 2, 8, q), jnp.float32),
            pltpu.SemaphoreType.DMA((19,)),
            pltpu.SemaphoreType.DMA((2 * SLOTS + 6,)),
        ],
        compiler_params=pltpu.CompilerParams(
            collective_id=0, has_side_effects=True, vmem_limit_bytes=32 * 2**20
        ),
        name="dedup",
    )(embeds, cluster.reshape(1, q))
    return top.reshape(q), mass.reshape(q)


def solution(mesh):
    return jax.shard_map(
        functools.partial(per_device, mesh.shape["docs"]),
        mesh=mesh,
        in_specs=(P(("docs", "rep"), None), P(("docs", "rep"))),
        out_specs=(P(("docs", "rep")), P(("docs", "rep"))),
        check_vma=False,
    )
```

```python
import functools
import math

import jax
import jax.numpy as jnp
from jax import lax
from jax.experimental import pallas as pl
from jax.experimental.pallas import tpu as pltpu
from jax.sharding import PartitionSpec as P

MESH = pl.DeviceIdType.MESH
dup_scale = 8.0
LOG2 = dup_scale * math.log2(math.e)
NO_PAIR = -100.0
REACH = 3
SLOTS = 2 * REACH + 1
OWN, ZA, ZB = REACH, SLOTS, SLOTS + 1
S_RES = 10
S_Z = S_RES + SLOTS
R_CORNER = SLOTS
R_RES = R_CORNER + 1
R_Z = R_RES + SLOTS + 3


def kernel(
    n,
    e_hbm,
    c_hbm,
    top_ref,
    mass_ref,
    e_ref,
    c_ref,
    buf,
    corner,
    xids,
    racc,
    cacc,
    rowres,
    rbuf,
    ssem,
    rsem,
    lsem,
):
    q, width = e_ref.shape
    half = q // 2
    d = lax.axis_index("docs")
    z = lax.axis_index("rep")
    odd = lax.rem(d, 2)
    corner_of_four = lax.rem(d, 4)
    low = corner_of_four < 2
    sis = 1 - 2 * odd
    near = jnp.where(low, 2, -2)
    far = 6 * odd - 3
    sister = d + sis
    to_a = jnp.where(z < 2, z + 2, 3 - z)
    from_a = jnp.where(z < 2, 3 - z, z - 2)
    mate = z + 1 - 2 * lax.rem(z, 2)
    inner = (z == 1) | (z == 2)
    outer = (z == 0) | (z == 3)

    def has(k):
        return (d + k >= 0) & (d + k < n)

    corner_in = (z == 0) & has(-4)
    corner_out = (z == 3) & has(4)
    ends = (corner_of_four == 0) | (corner_of_four == 3)

    def remote(src, dst, s, r, dev):
        return pltpu.make_async_remote_copy(
            src_ref=src,
            dst_ref=dst,
            send_sem=ssem.at[s],
            recv_sem=rsem.at[r],
            device_id=dev,
            device_id_type=MESH,
        )

    barrier = pltpu.get_barrier_semaphore()

    def greet(dev):
        pl.semaphore_signal(barrier, inc=1, device_id=dev, device_id_type=MESH)

    load_e = pltpu.make_async_copy(e_hbm, e_ref, lsem.at[0])
    load_c = pltpu.make_async_copy(c_hbm, c_ref, lsem.at[1])
    load_e.start()
    load_c.start()
    total = jnp.int32(3)
    for k in (-3, -2, -1, 1, 2, 3):
        pl.when(has(k))(functools.partial(greet, (d + k, z)))
        total = total + has(k).astype(jnp.int32)
    for k in (-4, 4):
        pl.when(has(k) & ends)(functools.partial(greet, (d + k, z)))
        total = total + (has(k) & ends).astype(jnp.int32)
    greet((d, to_a))
    greet((d, from_a))
    greet((d, mate))
    pl.when(corner_in)(functools.partial(greet, (d - 4, 3)))
    pl.when(corner_out)(functools.partial(greet, (d + 4, 0)))
    total = total + corner_in.astype(jnp.int32) + corner_out.astype(jnp.int32)

    own = buf.at[OWN]
    id_rows = pl.ds(q, 16)

    def z_copy(part, slot, dev):
        first = 3 * (slot - ZA)
        if part == 2:
            view = (id_rows, pl.ds(0, q))
        else:
            view = (pl.ds(part * half, half),)
        return remote(
            buf.at[(OWN,) + view],
            buf.at[(slot,) + view],
            S_Z + first + part,
            R_Z + first + part,
            dev,
        )

    def send_z(part):
        z_copy(part, ZA, (d, to_a)).start()
        pl.when(outer)(z_copy(part, ZB, (d, mate)).start)

    load_c.wait()
    ids = c_ref[...].astype(jnp.float32)
    buf[OWN, q : q + 16, :] = jnp.zeros((16, width), jnp.bfloat16)
    buf[OWN, q : q + 16, 0:q] = jnp.broadcast_to(ids, (16, q)).astype(jnp.bfloat16)
    load_e.wait()
    for part in range(2):
        rows = pl.ds(part * half, half)
        x = e_ref[rows, :].astype(jnp.float32)
        scale = lax.rsqrt(jnp.mean(x * x, axis=1, keepdims=True) + 1e-06)
        buf[OWN, rows, :] = (x * scale * width ** (-0.5)).astype(jnp.bfloat16)
        if part == 0:
            pl.semaphore_wait(barrier, total)
            send_z(2)
        send_z(part)

    send_near = remote(own, buf.at[REACH - near], 0, REACH - near, (d + near, z))
    send_far = remote(own, buf.at[REACH - far], 1, REACH - far, (d + far, z))
    send_sis = remote(own, buf.at[REACH - sis], 2, REACH - sis, (sister, z))
    has_far = has(far)
    tail = pl.ds(q - 16, 32)
    send_corner = remote(buf.at[OWN, tail], corner, 3, R_CORNER, (d + 4, 0))
    pl.when(has_far)(send_far.start)
    send_near.start()
    send_sis.start()
    pl.when(corner_out)(send_corner.start)

    lanes = lax.broadcasted_iota(jnp.int32, (8, q), 1)
    subs = lax.broadcasted_iota(jnp.int32, (8, q), 0)

    def take_ids(slot):
        return buf[slot, q : q + 16, 0:q].astype(jnp.float32)[0:1]

    def load_x(slot):
        xids[...] = jnp.broadcast_to(take_ids(slot), (128, q)).T

    def clear_rows():
        racc[0] = jnp.full((q, 128), -1.0, jnp.float32)
        racc[1] = jnp.zeros((q, 128), jnp.float32)

    def tile(xslot, start, size, slot, diagonal=False):
        rows = pl.ds(start, size)
        scores = lax.dot_general(
            buf[xslot, rows, :],
            buf[slot, 0:q, :],
            (((1,), (1,)), ((), ())),
            preferred_element_type=jnp.float32,
        )
        yid = take_ids(slot)
        xid = xids[rows, :]
        tops, masses = [], []
        for lo in range(0, q, 128):
            mask = xid == yid[:, lo : lo + 128]
            if diagonal:
                i = lax.broadcasted_iota(jnp.int32, (size, 128), 0)
                j = lax.broadcasted_iota(jnp.int32, (size, 128), 1) + lo
                mask = mask & (i != j)
            top = jnp.where(mask, scores[:, lo : lo + 128], NO_PAIR)
            mass = jnp.exp2(top * LOG2 - LOG2)
            cols = pl.ds(lo, 128)
            cacc[slot, 0, :, cols] = jnp.maximum(
                cacc[slot, 0, :, cols], jnp.max(top.reshape(size // 8, 8, 128), axis=0)
            )
            cacc[slot, 1, :, cols] += jnp.sum(mass.reshape(size // 8, 8, 128), axis=0)
            tops.append(top)
            masses.append(mass)
        if not diagonal:
            racc[0, rows, :] = jnp.maximum(racc[0, rows, :], functools.reduce(jnp.maximum, tops))
            racc[1, rows, :] += functools.reduce(jnp.add, masses)

    def row_result(xi, start, size):
        rows = pl.ds(start, size)
        rowres[xi, 0, :, rows] = jnp.max(racc[0, rows, :].T.reshape(16, 8, size), axis=0)
        rowres[xi, 1, :, rows] = jnp.sum(racc[1, rows, :].T.reshape(16, 8, size), axis=0)

    cacc[:, 0] = jnp.full((SLOTS, 8, q), -1.0, jnp.float32)
    cacc[:, 1] = jnp.zeros((SLOTS, 8, q), jnp.float32)

    load_x(OWN)
    clear_rows()
    tile(OWN, 0, q, OWN, diagonal=True)

    def arrived(slot):
        remote(own, buf.at[slot], 0, slot, (sister, z)).wait_recv()

    across = jnp.where(low, 4 - 3 * odd, -1 - 3 * odd)
    across_from = jnp.where(low, 2 + odd, -3 + odd)
    has_across = has(across) & has(across_from)

    def go_on(slot, s, by):
        to = slot - by
        return remote(buf.at[slot], buf.at[to], s, to, (d + by, z))

    go_across = go_on(REACH + across_from, 4, across)
    go_near = go_on(REACH + near, 5, sis)
    go_diag = go_on(REACH - near, 6, sis)
    has_diag = has(-near)

    @pl.when(has_far)
    def _():
        arrived(REACH + far)

    pl.when(has_across & jnp.logical_not(ends))(go_across.start)
    arrived(REACH + near)
    go_near.start()
    pl.when(has_across & ends)(go_across.start)
    arrived(REACH + sis)

    order = (0, sis, near, far, near + sis, -near, -near + sis)

    def nth(i):
        k = jnp.int32(0)
        for j in range(1, SLOTS):
            k = jnp.where(i == j, order[j], k)
        return k

    def own_step(i, carry):
        k = nth(i)

        @pl.when((k > 0) & has(k))
        def _():
            tile(OWN, 0, q, REACH + k)

        return carry

    lax.fori_loop(1, 4, own_step, 0)

    @pl.when(has_diag)
    def _():
        arrived(REACH - near)
        go_diag.start()

    pl.when(has(near + sis))(functools.partial(arrived, REACH + near + sis))
    pl.when(has(-near + sis))(functools.partial(arrived, REACH - near + sis))
    lax.fori_loop(4, SLOTS, own_step, 0)
    row_result(0, 0, q)
    clear_rows()

    def other_half(slot, xi, part, dev):
        if part == 0:
            z_copy(2, slot, dev).wait_recv()
        load_x(slot)
        z_copy(part, slot, dev).wait_recv()

        def step(i, carry):
            @pl.when(has(i - REACH))
            def _():
                tile(slot, part * half, half, i)

            return carry

        lax.fori_loop(0, SLOTS, step, 0)
        row_result(xi, part * half, half)

    row_a = remote(rowres.at[1], rbuf.at[ZA], 7, R_RES + ZA, (d, from_a))
    row_b = remote(rowres.at[2], rbuf.at[ZB], 8, R_RES + ZB, (d, mate))

    other_half(ZA, 1, 0, (d, from_a))

    @pl.when(inner)
    def _():
        clear_rows()
        other_half(ZB, 2, 0, (d, mate))
        other_half(ZB, 2, 1, (d, mate))
        row_b.start()
        clear_rows()

    other_half(ZA, 1, 1, (d, from_a))
    row_a.start()

    back = remote(rowres.at[3], rbuf.at[SLOTS + 2], 9, R_RES + SLOTS + 2, (d - 4, 3))

    @pl.when(corner_in)
    def _():
        remote(buf.at[OWN, tail], corner, 3, R_CORNER, (d - 4, 3)).wait_recv()
        first = buf[OWN, 0:16, :].astype(jnp.float32)[0:1]
        last = corner[0:16, :].astype(jnp.float32)[15:16]
        cos = jnp.sum(first * last, axis=1, keepdims=True)
        here = take_ids(OWN)[:, 0:1]
        there = corner[16:32, 0:q].astype(jnp.float32)[0:1, q - 1 : q]
        top = jnp.broadcast_to(jnp.where(here == there, cos, NO_PAIR), (8, q))
        mass = jnp.exp2(top * LOG2 - LOG2)
        mine = (lanes == 0) & (subs == 0)
        cacc[OWN, 0] = jnp.maximum(cacc[OWN, 0], jnp.where(mine, top, -1.0))
        cacc[OWN, 1] += jnp.where(mine, mass, 0.0)
        theirs = (lanes == q - 1) & (subs == 0)
        rowres[3, 0] = jnp.where(theirs, top, -1.0)
        rowres[3, 1] = jnp.where(theirs, mass, 0.0)
        back.start()

    def result(k):
        return remote(
            cacc.at[REACH + k],
            rbuf.at[REACH - k],
            S_RES + REACH + k,
            R_RES + REACH - k,
            (d + k, z),
        )

    for k in (-3, -2, -1, 1, 2, 3):
        pl.when(has(k))(result(k).start)

    top_ref[...] = jnp.max(jnp.maximum(rowres[0, 0], cacc[OWN, 0]), axis=0, keepdims=True)
    mass_ref[...] = jnp.sum(rowres[0, 1] + cacc[OWN, 1], axis=0, keepdims=True)

    def add_result(slot):
        remote(rowres.at[0], rbuf.at[slot], 7, R_RES + slot, (sister, z)).wait_recv()
        top_ref[...] = jnp.maximum(
            top_ref[...], jnp.max(rbuf[slot, 0], axis=0, keepdims=True)
        )
        mass_ref[...] += jnp.sum(rbuf[slot, 1], axis=0, keepdims=True)

    pl.when(corner_out)(functools.partial(add_result, SLOTS + 2))
    for k in (-3, -2, -1, 1, 2, 3):
        pl.when(has(k))(functools.partial(add_result, REACH + k))
    add_result(ZA)
    pl.when(outer)(functools.partial(add_result, ZB))

    for part in range(3):
        z_copy(part, ZA, (d, to_a)).wait_send()
        pl.when(outer)(z_copy(part, ZB, (d, mate)).wait_send)
    send_near.wait_send()
    pl.when(has_far)(send_far.wait_send)
    send_sis.wait_send()
    pl.when(corner_out)(send_corner.wait_send)
    pl.when(has_across)(go_across.wait_send)
    go_near.wait_send()
    pl.when(has_diag)(go_diag.wait_send)
    for k in (-3, -2, -1, 1, 2, 3):
        pl.when(has(k))(result(k).wait_send)
    row_a.wait_send()
    pl.when(inner)(row_b.wait_send)
    pl.when(corner_in)(back.wait_send)


def per_device(n, embeds, cluster):
    q, width = embeds.shape
    top, mass = pl.pallas_call(
        functools.partial(kernel, n),
        out_shape=(jax.ShapeDtypeStruct((1, q), jnp.float32),) * 2,
        in_specs=[pl.BlockSpec(memory_space=pltpu.HBM)] * 2,
        out_specs=(pl.BlockSpec(memory_space=pltpu.VMEM),) * 2,
        scratch_shapes=[
            pltpu.VMEM((q, width), jnp.bfloat16),
            pltpu.VMEM((1, q), jnp.int32),
            pltpu.VMEM((SLOTS + 2, q + 16, width), jnp.bfloat16),
            pltpu.VMEM((32, width), jnp.bfloat16),
            pltpu.VMEM((q, 128), jnp.float32),
            pltpu.VMEM((2, q, 128), jnp.float32),
            pltpu.VMEM((SLOTS, 2, 8, q), jnp.float32),
            pltpu.VMEM((4, 2, 8, q), jnp.float32),
            pltpu.VMEM((SLOTS + 3, 2, 8, q), jnp.float32),
            pltpu.SemaphoreType.DMA((S_Z + 6,)),
            pltpu.SemaphoreType.DMA((R_Z + 6,)),
            pltpu.SemaphoreType.DMA((2,)),
        ],
        compiler_params=pltpu.CompilerParams(
            collective_id=0, has_side_effects=True, vmem_limit_bytes=32 * 2**20
        ),
        name="dedup",
    )(embeds, cluster.reshape(1, q))
    return top.reshape(q), mass.reshape(q)


def solution(mesh):
    return jax.shard_map(
        functools.partial(per_device, mesh.shape["docs"]),
        mesh=mesh,
        in_specs=(P(("docs", "rep"), None), P(("docs", "rep"))),
        out_specs=(P(("docs", "rep")), P(("docs", "rep"))),
        check_vma=False,
    )
```

```python
import functools
import math

import jax
import jax.numpy as jnp
from jax import lax
from jax.experimental import pallas as pl
from jax.experimental.pallas import tpu as pltpu
from jax.sharding import PartitionSpec as P

MESH = pl.DeviceIdType.MESH
dup_scale = 8.0
LOG2 = dup_scale * math.log2(math.e)
NO_PAIR = -100.0
REACH = 3
SLOTS = 2 * REACH + 1
OWN, ZA, ZB = REACH, SLOTS, SLOTS + 1
S_CORNER = 12
S_ROW = S_CORNER + 1
S_RES = S_ROW + 3
S_Z = S_RES + SLOTS
R_CORNER = 2 * SLOTS
R_RES = R_CORNER + 1
R_Z = R_RES + SLOTS + 3


def kernel(
    n,
    e_hbm,
    c_hbm,
    top_ref,
    mass_ref,
    e_ref,
    c_ref,
    buf,
    corner,
    xids,
    racc,
    cacc,
    rowres,
    rbuf,
    ssem,
    rsem,
    lsem,
):
    q, width = e_ref.shape
    half = q // 2
    d = lax.axis_index("docs")
    z = lax.axis_index("rep")
    odd = lax.rem(d, 2)
    corner_of_four = lax.rem(d, 4)
    low = corner_of_four < 2
    sis = 1 - 2 * odd
    near = jnp.where(low, 2, -2)
    far = 6 * odd - 3
    sister = d + sis
    to_a = jnp.where(z < 2, z + 2, 3 - z)
    from_a = jnp.where(z < 2, 3 - z, z - 2)
    mate = z + 1 - 2 * lax.rem(z, 2)
    inner = (z == 1) | (z == 2)
    outer = (z == 0) | (z == 3)

    def has(k):
        return (d + k >= 0) & (d + k < n)

    corner_in = (z == 0) & has(-4)
    corner_out = (z == 3) & has(4)
    ends = (corner_of_four == 0) | (corner_of_four == 3)

    def remote(src, dst, s, r, dev):
        return pltpu.make_async_remote_copy(
            src_ref=src,
            dst_ref=dst,
            send_sem=ssem.at[s],
            recv_sem=rsem.at[r],
            device_id=dev,
            device_id_type=MESH,
        )

    barrier = pltpu.get_barrier_semaphore()

    def greet(dev):
        pl.semaphore_signal(barrier, inc=1, device_id=dev, device_id_type=MESH)

    load_e = pltpu.make_async_copy(e_hbm, e_ref, lsem.at[0])
    load_c = pltpu.make_async_copy(c_hbm, c_ref, lsem.at[1])
    load_e.start()
    load_c.start()
    total = jnp.int32(3)
    for k in (-3, -2, -1, 1, 2, 3):
        pl.when(has(k))(functools.partial(greet, (d + k, z)))
        total = total + has(k).astype(jnp.int32)
    for k in (-4, 4):
        pl.when(has(k) & ends)(functools.partial(greet, (d + k, z)))
        total = total + (has(k) & ends).astype(jnp.int32)
    greet((d, to_a))
    greet((d, from_a))
    greet((d, mate))
    pl.when(corner_in)(functools.partial(greet, (d - 4, 3)))
    pl.when(corner_out)(functools.partial(greet, (d + 4, 0)))
    total = total + corner_in.astype(jnp.int32) + corner_out.astype(jnp.int32)

    id_rows = pl.ds(q, 16)

    def z_copy(part, slot, dev):
        first = 3 * (slot - ZA)
        if part == 2:
            view = (id_rows, pl.ds(0, q))
        else:
            view = (pl.ds(part * half, half),)
        return remote(
            buf.at[(OWN,) + view],
            buf.at[(slot,) + view],
            S_Z + first + part,
            R_Z + first + part,
            dev,
        )

    def send_z(part):
        pl.when(outer)(z_copy(part, ZB, (d, mate)).start)
        z_copy(part, ZA, (d, to_a)).start()

    def halves(slot, to, s, dev):
        return [
            remote(buf.at[slot, view], buf.at[to, view], 2 * s + part, 2 * to + part, dev)
            for part, view in enumerate((pl.ds(0, half), pl.ds(half, half + 16)))
        ]

    send_near = halves(OWN, REACH - near, 0, (d + near, z))
    send_far = halves(OWN, REACH - far, 1, (d + far, z))
    send_sis = halves(OWN, REACH - sis, 2, (sister, z))
    has_far = has(far)
    tail = pl.ds(q - 16, 32)
    send_corner = remote(buf.at[OWN, tail], corner, S_CORNER, R_CORNER, (d + 4, 0))

    load_c.wait()
    ids = c_ref[...].astype(jnp.float32)
    buf[OWN, q : q + 16, :] = jnp.zeros((16, width), jnp.bfloat16)
    buf[OWN, q : q + 16, 0:q] = jnp.broadcast_to(ids, (16, q)).astype(jnp.bfloat16)
    load_e.wait()
    for part in range(2):
        rows = pl.ds(part * half, half)
        x = e_ref[rows, :].astype(jnp.float32)
        scale = lax.rsqrt(jnp.mean(x * x, axis=1, keepdims=True) + 1e-06)
        buf[OWN, rows, :] = (x * scale * width ** (-0.5)).astype(jnp.bfloat16)
        if part == 0:
            pl.semaphore_wait(barrier, total)
        pl.when(has_far)(send_far[part].start)
        send_near[part].start()
        send_z(part)
        send_sis[part].start()
        if part == 0:
            send_z(2)
    pl.when(corner_out)(send_corner.start)

    lanes = lax.broadcasted_iota(jnp.int32, (8, q), 1)
    subs = lax.broadcasted_iota(jnp.int32, (8, q), 0)

    def take_ids(slot):
        return buf[slot, q : q + 16, 0:q].astype(jnp.float32)[0:1]

    def load_x(slot):
        xids[...] = jnp.broadcast_to(take_ids(slot), (128, q)).T

    def clear_rows():
        racc[0] = jnp.full((q, 128), -1.0, jnp.float32)
        racc[1] = jnp.zeros((q, 128), jnp.float32)

    def tile(xslot, start, size, slot, diagonal=False):
        rows = pl.ds(start, size)
        scores = lax.dot_general(
            buf[xslot, rows, :],
            buf[slot, 0:q, :],
            (((1,), (1,)), ((), ())),
            preferred_element_type=jnp.float32,
        )
        yid = take_ids(slot)
        xid = xids[rows, :]
        tops, masses = [], []
        for lo in range(0, q, 128):
            mask = xid == yid[:, lo : lo + 128]
            if diagonal:
                i = lax.broadcasted_iota(jnp.int32, (size, 128), 0)
                j = lax.broadcasted_iota(jnp.int32, (size, 128), 1) + lo
                mask = mask & (i != j)
            top = jnp.where(mask, scores[:, lo : lo + 128], NO_PAIR)
            mass = jnp.exp2(top * LOG2 - LOG2)
            cols = pl.ds(lo, 128)
            cacc[slot, 0, :, cols] = jnp.maximum(
                cacc[slot, 0, :, cols], jnp.max(top.reshape(size // 8, 8, 128), axis=0)
            )
            cacc[slot, 1, :, cols] += jnp.sum(mass.reshape(size // 8, 8, 128), axis=0)
            tops.append(top)
            masses.append(mass)
        if not diagonal:
            racc[0, rows, :] = jnp.maximum(racc[0, rows, :], functools.reduce(jnp.maximum, tops))
            racc[1, rows, :] += functools.reduce(jnp.add, masses)

    def row_result(xi, start, size):
        rows = pl.ds(start, size)
        rowres[xi, 0, :, rows] = jnp.max(racc[0, rows, :].T.reshape(16, 8, size), axis=0)
        rowres[xi, 1, :, rows] = jnp.sum(racc[1, rows, :].T.reshape(16, 8, size), axis=0)

    cacc[:, 0] = jnp.full((SLOTS, 8, q), -1.0, jnp.float32)
    cacc[:, 1] = jnp.zeros((SLOTS, 8, q), jnp.float32)

    load_x(OWN)
    clear_rows()
    tile(OWN, 0, q, OWN, diagonal=True)

    def arrived(slot, parts=(0, 1)):
        copies = halves(OWN, slot, 0, (sister, z))
        for part in parts:
            copies[part].wait_recv()

    across = jnp.where(low, 4 - 3 * odd, -1 - 3 * odd)
    across_from = jnp.where(low, 2 + odd, -3 + odd)
    has_across = has(across) & has(across_from)

    def go_on(slot, s, by):
        return halves(slot, slot - by, s, (d + by, z))

    go_across = go_on(REACH + across_from, 3, across)
    go_near = go_on(REACH + near, 4, sis)
    go_diag = go_on(REACH - near, 5, sis)
    has_diag = has(-near)

    for part in range(2):
        pl.when(has_far)(functools.partial(arrived, REACH + far, (part,)))
        pl.when(has_across & jnp.logical_not(ends))(go_across[part].start)
        arrived(REACH + near, (part,))
        pl.when(has_across & ends)(go_across[part].start)
        go_near[part].start()
    arrived(REACH + sis)

    order = (0, sis, near, far, near + sis, -near, -near + sis)

    def nth(i):
        k = jnp.int32(0)
        for j in range(1, SLOTS):
            k = jnp.where(i == j, order[j], k)
        return k

    def own_step(i, carry):
        k = nth(i)

        @pl.when((k > 0) & has(k))
        def _():
            tile(OWN, 0, q, REACH + k)

        return carry

    lax.fori_loop(1, 4, own_step, 0)

    @pl.when(has_diag)
    def _():
        for part in range(2):
            arrived(REACH - near, (part,))
            go_diag[part].start()

    pl.when(has(near + sis))(functools.partial(arrived, REACH + near + sis))
    pl.when(has(-near + sis))(functools.partial(arrived, REACH - near + sis))
    lax.fori_loop(4, SLOTS, own_step, 0)
    row_result(0, 0, q)
    clear_rows()

    def result(k):
        return remote(
            cacc.at[REACH + k],
            rbuf.at[REACH - k],
            S_RES + REACH + k,
            R_RES + REACH - k,
            (d + k, z),
        )

    def other_half(slot, xi, part, xz, dev, last=False):
        if part == 0:
            z_copy(2, slot, dev).wait_recv()
        load_x(slot)
        z_copy(part, slot, dev).wait_recv()

        def step(i, carry):
            k = i - REACH
            apart = ((k == REACH) & (xz < z - 1)) | ((k == -REACH) & (z < xz - 1))

            @pl.when(has(k) & jnp.logical_not(apart))
            def _():
                tile(slot, part * half, half, i)

            if last:
                pl.when(has(k) & (k != 0))(lambda: result(k).start())
            return carry

        lax.fori_loop(0, SLOTS, step, 0)
        row_result(xi, part * half, half)

    row_a = remote(rowres.at[1], rbuf.at[ZA], S_ROW, R_RES + ZA, (d, from_a))
    row_b = remote(rowres.at[2], rbuf.at[ZB], S_ROW + 1, R_RES + ZB, (d, mate))

    @pl.when(inner)
    def _():
        other_half(ZB, 2, 0, mate, (d, mate))
        other_half(ZB, 2, 1, mate, (d, mate))
        row_b.start()
        clear_rows()

    other_half(ZA, 1, 0, from_a, (d, from_a))
    other_half(ZA, 1, 1, from_a, (d, from_a), last=True)
    row_a.start()

    back = remote(rowres.at[3], rbuf.at[SLOTS + 2], S_ROW + 2, R_RES + SLOTS + 2, (d - 4, 3))

    @pl.when(corner_in)
    def _():
        remote(buf.at[OWN, tail], corner, S_CORNER, R_CORNER, (d - 4, 3)).wait_recv()
        first = buf[OWN, 0:16, :].astype(jnp.float32)[0:1]
        last = corner[0:16, :].astype(jnp.float32)[15:16]
        cos = jnp.sum(first * last, axis=1, keepdims=True)
        here = take_ids(OWN)[:, 0:1]
        there = corner[16:32, 0:q].astype(jnp.float32)[0:1, q - 1 : q]
        top = jnp.broadcast_to(jnp.where(here == there, cos, NO_PAIR), (8, q))
        mass = jnp.exp2(top * LOG2 - LOG2)
        mine = (lanes == 0) & (subs == 0)
        cacc[OWN, 0] = jnp.maximum(cacc[OWN, 0], jnp.where(mine, top, -1.0))
        cacc[OWN, 1] += jnp.where(mine, mass, 0.0)
        theirs = (lanes == q - 1) & (subs == 0)
        rowres[3, 0] = jnp.where(theirs, top, -1.0)
        rowres[3, 1] = jnp.where(theirs, mass, 0.0)
        back.start()

    top_ref[...] = jnp.max(jnp.maximum(rowres[0, 0], cacc[OWN, 0]), axis=0, keepdims=True)
    mass_ref[...] = jnp.sum(rowres[0, 1] + cacc[OWN, 1], axis=0, keepdims=True)

    def add_result(slot):
        remote(rowres.at[0], rbuf.at[slot], S_ROW, R_RES + slot, (sister, z)).wait_recv()
        top_ref[...] = jnp.maximum(
            top_ref[...], jnp.max(rbuf[slot, 0], axis=0, keepdims=True)
        )
        mass_ref[...] += jnp.sum(rbuf[slot, 1], axis=0, keepdims=True)

    pl.when(corner_out)(functools.partial(add_result, SLOTS + 2))
    for k in (-3, -2, -1, 1, 2, 3):
        pl.when(has(k))(functools.partial(add_result, REACH + k))
    add_result(ZA)
    pl.when(outer)(functools.partial(add_result, ZB))

    for part in range(3):
        z_copy(part, ZA, (d, to_a)).wait_send()
        pl.when(outer)(z_copy(part, ZB, (d, mate)).wait_send)
    for part in range(2):
        send_near[part].wait_send()
        pl.when(has_far)(send_far[part].wait_send)
        send_sis[part].wait_send()
        pl.when(has_across)(go_across[part].wait_send)
        go_near[part].wait_send()
        pl.when(has_diag)(go_diag[part].wait_send)
    pl.when(corner_out)(send_corner.wait_send)
    for k in (-3, -2, -1, 1, 2, 3):
        pl.when(has(k))(result(k).wait_send)
    row_a.wait_send()
    pl.when(inner)(row_b.wait_send)
    pl.when(corner_in)(back.wait_send)


def per_device(n, embeds, cluster):
    q, width = embeds.shape
    top, mass = pl.pallas_call(
        functools.partial(kernel, n),
        out_shape=(jax.ShapeDtypeStruct((1, q), jnp.float32),) * 2,
        in_specs=[pl.BlockSpec(memory_space=pltpu.HBM)] * 2,
        out_specs=(pl.BlockSpec(memory_space=pltpu.VMEM),) * 2,
        scratch_shapes=[
            pltpu.VMEM((q, width), jnp.bfloat16),
            pltpu.VMEM((1, q), jnp.int32),
            pltpu.VMEM((SLOTS + 2, q + 16, width), jnp.bfloat16),
            pltpu.VMEM((32, width), jnp.bfloat16),
            pltpu.VMEM((q, 128), jnp.float32),
            pltpu.VMEM((2, q, 128), jnp.float32),
            pltpu.VMEM((SLOTS, 2, 8, q), jnp.float32),
            pltpu.VMEM((4, 2, 8, q), jnp.float32),
            pltpu.VMEM((SLOTS + 3, 2, 8, q), jnp.float32),
            pltpu.SemaphoreType.DMA((S_Z + 6,)),
            pltpu.SemaphoreType.DMA((R_Z + 6,)),
            pltpu.SemaphoreType.DMA((2,)),
        ],
        compiler_params=pltpu.CompilerParams(
            collective_id=0, has_side_effects=True, vmem_limit_bytes=63 * 2**20
        ),
        name="dedup",
    )(embeds, cluster.reshape(1, q))
    return top.reshape(q), mass.reshape(q)


def solution(mesh):
    return jax.shard_map(
        functools.partial(per_device, mesh.shape["docs"]),
        mesh=mesh,
        in_specs=(P(("docs", "rep"), None), P(("docs", "rep"))),
        out_specs=(P(("docs", "rep")), P(("docs", "rep"))),
        check_vma=False,
    )
```

```python
import functools
import math

import jax
import jax.numpy as jnp
from jax import lax
from jax.experimental import pallas as pl
from jax.experimental.pallas import tpu as pltpu
from jax.sharding import PartitionSpec as P

MESH = pl.DeviceIdType.MESH
dup_scale = 8.0
LOG2 = dup_scale * math.log2(math.e)
NO_PAIR = -100.0
REACH = 3
SLOTS = 2 * REACH + 1
OWN, ZA, ZB = REACH, SLOTS, SLOTS + 1
S_CORNER = 12
S_ROW = S_CORNER + 1
S_RES = S_ROW + 3
S_Z = S_RES + SLOTS
R_CORNER = 2 * SLOTS
R_RES = R_CORNER + 1
R_Z = R_RES + SLOTS + 3


def kernel(
    n,
    e_hbm,
    c_hbm,
    out_ref,
    e_ref,
    c_ref,
    buf,
    corner,
    xids,
    racc,
    cacc,
    rowres,
    rbuf,
    ssem,
    rsem,
    lsem,
):
    q, width = e_ref.shape
    half = q // 2
    d = lax.axis_index("docs")
    z = lax.axis_index("rep")
    odd = lax.rem(d, 2)
    corner_of_four = lax.rem(d, 4)
    low = corner_of_four < 2
    sis = 1 - 2 * odd
    near = jnp.where(low, 2, -2)
    far = 6 * odd - 3
    sister = d + sis
    to_a = jnp.where(z < 2, z + 2, 3 - z)
    from_a = jnp.where(z < 2, 3 - z, z - 2)
    mate = z + 1 - 2 * lax.rem(z, 2)
    inner = (z == 1) | (z == 2)
    outer = (z == 0) | (z == 3)

    def has(k):
        return (d + k >= 0) & (d + k < n)

    corner_in = (z == 0) & has(-4)
    corner_out = (z == 3) & has(4)
    ends = (corner_of_four == 0) | (corner_of_four == 3)

    def remote(src, dst, s, r, dev):
        return pltpu.make_async_remote_copy(
            src_ref=src,
            dst_ref=dst,
            send_sem=ssem.at[s],
            recv_sem=rsem.at[r],
            device_id=dev,
            device_id_type=MESH,
        )

    barrier = pltpu.get_barrier_semaphore()

    def greet(dev):
        pl.semaphore_signal(barrier, inc=1, device_id=dev, device_id_type=MESH)

    load_e = pltpu.make_async_copy(e_hbm, e_ref, lsem.at[0])
    load_c = pltpu.make_async_copy(c_hbm, c_ref, lsem.at[1])
    load_e.start()
    load_c.start()
    total = jnp.int32(3)
    for k in (-3, -2, -1, 1, 2, 3):
        pl.when(has(k))(functools.partial(greet, (d + k, z)))
        total = total + has(k).astype(jnp.int32)
    for k in (-4, 4):
        pl.when(has(k) & ends)(functools.partial(greet, (d + k, z)))
        total = total + (has(k) & ends).astype(jnp.int32)
    greet((d, to_a))
    greet((d, from_a))
    greet((d, mate))
    pl.when(corner_in)(functools.partial(greet, (d - 4, 3)))
    pl.when(corner_out)(functools.partial(greet, (d + 4, 0)))
    total = total + corner_in.astype(jnp.int32) + corner_out.astype(jnp.int32)

    id_rows = pl.ds(q, 16)

    def z_copy(part, slot, dev):
        first = 3 * (slot - ZA)
        if part == 2:
            view = (id_rows, pl.ds(0, q))
        else:
            view = (pl.ds(part * half, half),)
        return remote(
            buf.at[(OWN,) + view],
            buf.at[(slot,) + view],
            S_Z + first + part,
            R_Z + first + part,
            dev,
        )

    def send_z(part):
        pl.when(outer)(z_copy(part, ZB, (d, mate)).start)
        z_copy(part, ZA, (d, to_a)).start()

    def halves(slot, to, s, dev):
        return [
            remote(buf.at[slot, view], buf.at[to, view], 2 * s + part, 2 * to + part, dev)
            for part, view in enumerate((pl.ds(0, half), pl.ds(half, half + 16)))
        ]

    send_near = halves(OWN, REACH - near, 0, (d + near, z))
    send_far = halves(OWN, REACH - far, 1, (d + far, z))
    send_sis = halves(OWN, REACH - sis, 2, (sister, z))
    has_far = has(far)
    tail = pl.ds(q - 16, 32)
    send_corner = remote(buf.at[OWN, tail], corner, S_CORNER, R_CORNER, (d + 4, 0))

    load_c.wait()
    ids = c_ref[...].astype(jnp.float32)
    buf[OWN, q : q + 16, :] = jnp.zeros((16, width), jnp.bfloat16)
    buf[OWN, q : q + 16, 0:q] = jnp.broadcast_to(ids, (16, q)).astype(jnp.bfloat16)
    load_e.wait()
    for part in range(2):
        rows = pl.ds(part * half, half)
        x = e_ref[rows, :].astype(jnp.float32)
        scale = lax.rsqrt(jnp.mean(x * x, axis=1, keepdims=True) + 1e-06)
        buf[OWN, rows, :] = (x * scale * width ** (-0.5)).astype(jnp.bfloat16)
        if part == 0:
            pl.semaphore_wait(barrier, total)
        pl.when(has_far)(send_far[part].start)
        send_near[part].start()
        send_z(part)
        send_sis[part].start()
        if part == 0:
            send_z(2)
    pl.when(corner_out)(send_corner.start)

    lanes = lax.broadcasted_iota(jnp.int32, (8, q), 1)
    subs = lax.broadcasted_iota(jnp.int32, (8, q), 0)

    def take_ids(slot):
        return buf[slot, q : q + 16, 0:q].astype(jnp.float32)[0:1]

    def load_x(slot, xi):
        xids[xi] = jnp.broadcast_to(take_ids(slot), (128, q)).T

    def tile(xslot, xi, start, size, slot, diagonal=False):
        rows = pl.ds(start, size)
        scores = lax.dot_general(
            buf[xslot, rows, :],
            buf[slot, 0:q, :],
            (((1,), (1,)), ((), ())),
            preferred_element_type=jnp.float32,
        )
        yid = take_ids(slot)
        xid = xids[xi, rows, :]
        tops, masses = [], []
        for lo in range(0, q, 128):
            mask = xid == yid[:, lo : lo + 128]
            if diagonal:
                i = lax.broadcasted_iota(jnp.int32, (size, 128), 0)
                j = lax.broadcasted_iota(jnp.int32, (size, 128), 1) + lo
                mask = mask & (i != j)
            top = jnp.where(mask, scores[:, lo : lo + 128], NO_PAIR)
            mass = jnp.exp2(top * LOG2 - LOG2)
            cols = pl.ds(lo, 128)
            cacc[slot, 0, :, cols] = jnp.maximum(
                cacc[slot, 0, :, cols], jnp.max(top.reshape(size // 8, 8, 128), axis=0)
            )
            cacc[slot, 1, :, cols] += jnp.sum(mass.reshape(size // 8, 8, 128), axis=0)
            tops.append(top)
            masses.append(mass)
        if not diagonal:
            racc[xi, 0, rows, :] = jnp.maximum(
                racc[xi, 0, rows, :], functools.reduce(jnp.maximum, tops)
            )
            racc[xi, 1, rows, :] += functools.reduce(jnp.add, masses)

    def row_result(xi, start, size):
        rows = pl.ds(start, size)
        rowres[xi, 0, :, rows] = jnp.max(racc[xi, 0, rows, :].T.reshape(16, 8, size), axis=0)
        rowres[xi, 1, :, rows] = jnp.sum(racc[xi, 1, rows, :].T.reshape(16, 8, size), axis=0)

    cacc[:, 0] = jnp.full((SLOTS, 8, q), -1.0, jnp.float32)
    cacc[:, 1] = jnp.zeros((SLOTS, 8, q), jnp.float32)

    racc[:, 0] = jnp.full((3, q, 128), -1.0, jnp.float32)
    racc[:, 1] = jnp.zeros((3, q, 128), jnp.float32)
    load_x(OWN, 0)
    tile(OWN, 0, 0, q, OWN, diagonal=True)

    def arrived(slot, parts=(0, 1)):
        copies = halves(OWN, slot, 0, (sister, z))
        for part in parts:
            copies[part].wait_recv()

    across = jnp.where(low, 4 - 3 * odd, -1 - 3 * odd)
    across_from = jnp.where(low, 2 + odd, -3 + odd)
    has_across = has(across) & has(across_from)

    def go_on(slot, s, by):
        return halves(slot, slot - by, s, (d + by, z))

    go_across = go_on(REACH + across_from, 3, across)
    go_near = go_on(REACH + near, 4, sis)
    go_diag = go_on(REACH - near, 5, sis)
    has_diag = has(-near)

    for part in range(2):
        pl.when(has_far)(functools.partial(arrived, REACH + far, (part,)))
        pl.when(has_across & jnp.logical_not(ends))(go_across[part].start)
        arrived(REACH + near, (part,))
        pl.when(has_across & ends)(go_across[part].start)
        go_near[part].start()
    arrived(REACH + sis)

    order = (0, sis, near, far, near + sis, -near, -near + sis)

    def nth(i):
        k = jnp.int32(0)
        for j in range(1, SLOTS):
            k = jnp.where(i == j, order[j], k)
        return k

    def own_step(i, carry):
        k = nth(i)

        @pl.when((k > 0) & has(k))
        def _():
            tile(OWN, 0, 0, q, REACH + k)

        return carry

    lax.fori_loop(1, 4, own_step, 0)

    def diag(part):
        @pl.when(has_diag)
        def _():
            arrived(REACH - near, (part,))
            go_diag[part].start()

    def result(k):
        return remote(
            cacc.at[REACH + k],
            rbuf.at[REACH - k],
            S_RES + REACH + k,
            R_RES + REACH - k,
            (d + k, z),
        )

    def meet(slot, xi, xz, start, size, first, stop, last=False):
        def step(i, carry):
            k = nth(i)
            apart = ((k == REACH) & (xz < z - 1)) | ((k == -REACH) & (z < xz - 1))

            @pl.when(has(k) & jnp.logical_not(apart))
            def _():
                tile(slot, xi, start, size, REACH + k)

            if last:
                pl.when(has(k) & (k != 0))(lambda: result(k).start())
            return carry

        lax.fori_loop(first, stop, step, 0)

    row_a = remote(rowres.at[1], rbuf.at[ZA], S_ROW, R_RES + ZA, (d, from_a))
    row_b = remote(rowres.at[2], rbuf.at[ZB], S_ROW + 1, R_RES + ZB, (d, mate))

    diag(0)

    @pl.when(inner)
    def _():
        z_copy(2, ZB, (d, mate)).wait_recv()
        load_x(ZB, 2)
        for part in range(2):
            z_copy(part, ZB, (d, mate)).wait_recv()
        meet(ZB, 2, mate, 0, q, 0, 4)

    diag(1)
    z_copy(2, ZA, (d, from_a)).wait_recv()
    load_x(ZA, 1)
    z_copy(0, ZA, (d, from_a)).wait_recv()
    meet(ZA, 1, from_a, 0, half, 0, 4)

    pl.when(has(near + sis))(functools.partial(arrived, REACH + near + sis))
    pl.when(has(-near + sis))(functools.partial(arrived, REACH - near + sis))
    lax.fori_loop(4, SLOTS, own_step, 0)
    row_result(0, 0, q)

    @pl.when(inner)
    def _():
        meet(ZB, 2, mate, 0, q, 4, SLOTS)
        row_result(2, 0, q)
        row_b.start()

    meet(ZA, 1, from_a, 0, half, 4, SLOTS)
    row_result(1, 0, half)
    z_copy(1, ZA, (d, from_a)).wait_recv()
    meet(ZA, 1, from_a, half, half, 0, SLOTS, last=True)
    row_result(1, half, half)
    row_a.start()

    back = remote(rowres.at[3], rbuf.at[SLOTS + 2], S_ROW + 2, R_RES + SLOTS + 2, (d - 4, 3))

    @pl.when(corner_in)
    def _():
        remote(buf.at[OWN, tail], corner, S_CORNER, R_CORNER, (d - 4, 3)).wait_recv()
        first = buf[OWN, 0:16, :].astype(jnp.float32)[0:1]
        last = corner[0:16, :].astype(jnp.float32)[15:16]
        cos = jnp.sum(first * last, axis=1, keepdims=True)
        here = take_ids(OWN)[:, 0:1]
        there = corner[16:32, 0:q].astype(jnp.float32)[0:1, q - 1 : q]
        top = jnp.broadcast_to(jnp.where(here == there, cos, NO_PAIR), (8, q))
        mass = jnp.exp2(top * LOG2 - LOG2)
        mine = (lanes == 0) & (subs == 0)
        cacc[OWN, 0] = jnp.maximum(cacc[OWN, 0], jnp.where(mine, top, -1.0))
        cacc[OWN, 1] += jnp.where(mine, mass, 0.0)
        theirs = (lanes == q - 1) & (subs == 0)
        rowres[3, 0] = jnp.where(theirs, top, -1.0)
        rowres[3, 1] = jnp.where(theirs, mass, 0.0)
        back.start()

    out_ref[0] = jnp.maximum(rowres[0, 0], cacc[OWN, 0])
    out_ref[1] = rowres[0, 1] + cacc[OWN, 1]

    def add_result(slot):
        remote(rowres.at[0], rbuf.at[slot], S_ROW, R_RES + slot, (sister, z)).wait_recv()
        out_ref[0] = jnp.maximum(out_ref[0], rbuf[slot, 0])
        out_ref[1] += rbuf[slot, 1]

    pl.when(corner_out)(functools.partial(add_result, SLOTS + 2))
    for k in (-3, -2, -1, 1, 2, 3):
        pl.when(has(k))(functools.partial(add_result, REACH + k))
    add_result(ZA)
    pl.when(outer)(functools.partial(add_result, ZB))

    for part in range(3):
        z_copy(part, ZA, (d, to_a)).wait_send()
        pl.when(outer)(z_copy(part, ZB, (d, mate)).wait_send)
    for part in range(2):
        send_near[part].wait_send()
        pl.when(has_far)(send_far[part].wait_send)
        send_sis[part].wait_send()
        pl.when(has_across)(go_across[part].wait_send)
        go_near[part].wait_send()
        pl.when(has_diag)(go_diag[part].wait_send)
    pl.when(corner_out)(send_corner.wait_send)
    for k in (-3, -2, -1, 1, 2, 3):
        pl.when(has(k))(result(k).wait_send)
    row_a.wait_send()
    pl.when(inner)(row_b.wait_send)
    pl.when(corner_in)(back.wait_send)


def finish(both_ref, top_ref, mass_ref):
    top_ref[...] = jnp.max(both_ref[0], axis=0)
    mass_ref[...] = jnp.sum(both_ref[1], axis=0)


def per_device(n, embeds, cluster):
    q, width = embeds.shape
    both = pl.pallas_call(
        functools.partial(kernel, n),
        out_shape=jax.ShapeDtypeStruct((2, 8, q), jnp.float32),
        in_specs=[pl.BlockSpec(memory_space=pltpu.HBM)] * 2,
        out_specs=pl.BlockSpec(memory_space=pltpu.VMEM),
        scratch_shapes=[
            pltpu.VMEM((q, width), jnp.bfloat16),
            pltpu.VMEM((1, q), jnp.int32),
            pltpu.VMEM((SLOTS + 2, q + 16, width), jnp.bfloat16),
            pltpu.VMEM((32, width), jnp.bfloat16),
            pltpu.VMEM((3, q, 128), jnp.float32),
            pltpu.VMEM((3, 2, q, 128), jnp.float32),
            pltpu.VMEM((SLOTS, 2, 8, q), jnp.float32),
            pltpu.VMEM((4, 2, 8, q), jnp.float32),
            pltpu.VMEM((SLOTS + 3, 2, 8, q), jnp.float32),
            pltpu.SemaphoreType.DMA((S_Z + 6,)),
            pltpu.SemaphoreType.DMA((R_Z + 6,)),
            pltpu.SemaphoreType.DMA((2,)),
        ],
        compiler_params=pltpu.CompilerParams(
            collective_id=0, has_side_effects=True, vmem_limit_bytes=63 * 2**20
        ),
        name="dedup",
    )(embeds, cluster.reshape(1, q))
    return pl.pallas_call(
        finish,
        out_shape=(jax.ShapeDtypeStruct((q,), jnp.float32),) * 2,
        in_specs=[pl.BlockSpec(memory_space=pltpu.VMEM)],
        out_specs=(pl.BlockSpec(memory_space=pltpu.VMEM),) * 2,
        name="finish",
    )(both)


def solution(mesh):
    return jax.shard_map(
        functools.partial(per_device, mesh.shape["docs"]),
        mesh=mesh,
        in_specs=(P(("docs", "rep"), None), P(("docs", "rep"))),
        out_specs=(P(("docs", "rep")), P(("docs", "rep"))),
        check_vma=False,
    )
```

```python
import functools
import math

import jax
import jax.numpy as jnp
from jax import lax
from jax.experimental import pallas as pl
from jax.experimental.pallas import tpu as pltpu
from jax.sharding import PartitionSpec as P

MESH = pl.DeviceIdType.MESH
dup_scale = 8.0
LOG2 = dup_scale * math.log2(math.e)
NO_PAIR = -100.0
REACH = 3
SLOTS = 2 * REACH + 1
OWN, ZA, ZB = REACH, SLOTS, SLOTS + 1
S_CORNER = 12
S_ROW = S_CORNER + 1
S_RES = S_ROW + 3
S_Z = S_RES + SLOTS
R_CORNER = 2 * SLOTS
R_RES = R_CORNER + 1
R_Z = R_RES + SLOTS + 3


def kernel(
    n,
    e_hbm,
    c_hbm,
    out_ref,
    e_ref,
    c_ref,
    buf,
    corner,
    xids,
    racc,
    cacc,
    rowres,
    rbuf,
    ssem,
    rsem,
    lsem,
):
    q, width = e_ref.shape
    half = q // 2
    most = 3 * q // 4
    d = lax.axis_index("docs")
    z = lax.axis_index("rep")
    odd = lax.rem(d, 2)
    corner_of_four = lax.rem(d, 4)
    low = corner_of_four < 2
    sis = 1 - 2 * odd
    near = jnp.where(low, 2, -2)
    far = 6 * odd - 3
    sister = d + sis
    to_a = jnp.where(z < 2, z + 2, 3 - z)
    from_a = jnp.where(z < 2, 3 - z, z - 2)
    mate = z + 1 - 2 * lax.rem(z, 2)
    inner = (z == 1) | (z == 2)
    outer = (z == 0) | (z == 3)

    def has(k):
        return (d + k >= 0) & (d + k < n)

    corner_in = (z == 0) & has(-4)
    corner_out = (z == 3) & has(4)
    ends = (corner_of_four == 0) | (corner_of_four == 3)

    def remote(src, dst, s, r, dev):
        return pltpu.make_async_remote_copy(
            src_ref=src,
            dst_ref=dst,
            send_sem=ssem.at[s],
            recv_sem=rsem.at[r],
            device_id=dev,
            device_id_type=MESH,
        )

    barrier = pltpu.get_barrier_semaphore()

    def greet(dev):
        pl.semaphore_signal(barrier, inc=1, device_id=dev, device_id_type=MESH)

    load_e = pltpu.make_async_copy(e_hbm, e_ref, lsem.at[0])
    load_c = pltpu.make_async_copy(c_hbm, c_ref, lsem.at[1])
    load_e.start()
    load_c.start()
    total = jnp.int32(3)
    for k in (-3, -2, -1, 1, 2, 3):
        pl.when(has(k))(functools.partial(greet, (d + k, z)))
        total = total + has(k).astype(jnp.int32)
    for k in (-4, 4):
        pl.when(has(k) & ends)(functools.partial(greet, (d + k, z)))
        total = total + (has(k) & ends).astype(jnp.int32)
    greet((d, to_a))
    greet((d, from_a))
    greet((d, mate))
    pl.when(corner_in)(functools.partial(greet, (d - 4, 3)))
    pl.when(corner_out)(functools.partial(greet, (d + 4, 0)))
    total = total + corner_in.astype(jnp.int32) + corner_out.astype(jnp.int32)

    id_rows = pl.ds(q, 16)

    def z_copy(part, slot, dev):
        first = 3 * (slot - ZA)
        if part == 2:
            view = (id_rows, pl.ds(0, q))
        else:
            view = (pl.ds(0, most) if part == 0 else pl.ds(most, q - most),)
        return remote(
            buf.at[(OWN,) + view],
            buf.at[(slot,) + view],
            S_Z + first + part,
            R_Z + first + part,
            dev,
        )

    def send_z(part):
        pl.when(outer)(z_copy(part, ZB, (d, mate)).start)
        z_copy(part, ZA, (d, to_a)).start()

    def halves(slot, to, s, dev):
        return [
            remote(buf.at[slot, view], buf.at[to, view], 2 * s + part, 2 * to + part, dev)
            for part, view in enumerate((pl.ds(0, half), pl.ds(half, half + 16)))
        ]

    send_near = halves(OWN, REACH - near, 0, (d + near, z))
    send_far = halves(OWN, REACH - far, 1, (d + far, z))
    send_sis = halves(OWN, REACH - sis, 2, (sister, z))
    has_far = has(far)
    tail = pl.ds(q - 16, 32)
    send_corner = remote(buf.at[OWN, tail], corner, S_CORNER, R_CORNER, (d + 4, 0))

    load_c.wait()
    ids = c_ref[...].astype(jnp.float32)
    buf[OWN, q : q + 16, :] = jnp.zeros((16, width), jnp.bfloat16)
    buf[OWN, q : q + 16, 0:q] = jnp.broadcast_to(ids, (16, q)).astype(jnp.bfloat16)
    load_e.wait()
    for part, rows in enumerate((pl.ds(0, most), pl.ds(most, q - most))):
        x = e_ref[rows, :].astype(jnp.float32)
        scale = lax.rsqrt(jnp.mean(x * x, axis=1, keepdims=True) + 1e-06)
        buf[OWN, rows, :] = (x * scale * width ** (-0.5)).astype(jnp.bfloat16)
        if part == 0:
            pl.semaphore_wait(barrier, total)
            send_z(2)
        send_z(part)
        send_near[part].start()
        pl.when(has_far)(send_far[part].start)
        send_sis[part].start()
    pl.when(corner_out)(send_corner.start)

    lanes = lax.broadcasted_iota(jnp.int32, (8, q), 1)
    subs = lax.broadcasted_iota(jnp.int32, (8, q), 0)

    def take_ids(slot):
        return buf[slot, q : q + 16, 0:q].astype(jnp.float32)[0:1]

    def load_x(slot, xi):
        xids[xi] = jnp.broadcast_to(take_ids(slot), (128, q)).T

    def tile(xslot, xi, start, size, slot, diagonal=False):
        rows = pl.ds(start, size)
        scores = lax.dot_general(
            buf[xslot, rows, :],
            buf[slot, 0:q, :],
            (((1,), (1,)), ((), ())),
            preferred_element_type=jnp.float32,
        )
        yid = take_ids(slot)
        xid = xids[xi, rows, :]
        tops, masses = [], []
        for lo in range(0, q, 128):
            mask = xid == yid[:, lo : lo + 128]
            if diagonal:
                i = lax.broadcasted_iota(jnp.int32, (size, 128), 0)
                j = lax.broadcasted_iota(jnp.int32, (size, 128), 1) + lo
                mask = mask & (i != j)
            top = jnp.where(mask, scores[:, lo : lo + 128], NO_PAIR)
            mass = jnp.exp2(top * LOG2 - LOG2)
            cols = pl.ds(lo, 128)
            cacc[slot, 0, :, cols] = jnp.maximum(
                cacc[slot, 0, :, cols], jnp.max(top.reshape(size // 8, 8, 128), axis=0)
            )
            cacc[slot, 1, :, cols] += jnp.sum(mass.reshape(size // 8, 8, 128), axis=0)
            tops.append(top)
            masses.append(mass)
        if not diagonal:
            racc[xi, 0, rows, :] = jnp.maximum(
                racc[xi, 0, rows, :], functools.reduce(jnp.maximum, tops)
            )
            racc[xi, 1, rows, :] += functools.reduce(jnp.add, masses)

    def row_result(xi, start, size):
        rows = pl.ds(start, size)
        rowres[xi, 0, :, rows] = jnp.max(racc[xi, 0, rows, :].T.reshape(16, 8, size), axis=0)
        rowres[xi, 1, :, rows] = jnp.sum(racc[xi, 1, rows, :].T.reshape(16, 8, size), axis=0)

    cacc[:, 0] = jnp.full((SLOTS, 8, q), -1.0, jnp.float32)
    cacc[:, 1] = jnp.zeros((SLOTS, 8, q), jnp.float32)

    racc[:, 0] = jnp.full((3, q, 128), -1.0, jnp.float32)
    racc[:, 1] = jnp.zeros((3, q, 128), jnp.float32)
    load_x(OWN, 0)
    tile(OWN, 0, 0, q, OWN, diagonal=True)

    def arrived(slot, parts=(0, 1)):
        copies = halves(OWN, slot, 0, (sister, z))
        for part in parts:
            copies[part].wait_recv()

    across = jnp.where(low, 4 - 3 * odd, -1 - 3 * odd)
    across_from = jnp.where(low, 2 + odd, -3 + odd)
    has_across = has(across) & has(across_from)

    def go_on(slot, s, by):
        return halves(slot, slot - by, s, (d + by, z))

    go_across = go_on(REACH + across_from, 3, across)
    go_near = go_on(REACH + near, 4, sis)
    go_diag = go_on(REACH - near, 5, sis)
    has_diag = has(-near)

    for part in range(2):
        pl.when(has_far)(functools.partial(arrived, REACH + far, (part,)))
        pl.when(has_across & jnp.logical_not(ends))(go_across[part].start)
        arrived(REACH + near, (part,))
        pl.when(has_across & ends)(go_across[part].start)
        go_near[part].start()
    arrived(REACH + sis)

    order = (0, sis, near, far, near + sis, -near, -near + sis)

    def nth(i):
        k = jnp.int32(0)
        for j in range(1, SLOTS):
            k = jnp.where(i == j, order[j], k)
        return k

    def own_step(i, carry):
        k = nth(i)

        @pl.when((k > 0) & has(k))
        def _():
            tile(OWN, 0, 0, q, REACH + k)

        return carry

    lax.fori_loop(1, 4, own_step, 0)

    def diag(part):
        @pl.when(has_diag)
        def _():
            arrived(REACH - near, (part,))
            go_diag[part].start()

    def result(k):
        return remote(
            cacc.at[REACH + k],
            rbuf.at[REACH - k],
            S_RES + REACH + k,
            R_RES + REACH - k,
            (d + k, z),
        )

    def meet(slot, xi, xz, start, size, first, stop, last=False):
        def step(i, carry):
            k = nth(i)
            apart = ((k == REACH) & (xz < z - 1)) | ((k == -REACH) & (z < xz - 1))

            @pl.when(has(k) & jnp.logical_not(apart))
            def _():
                tile(slot, xi, start, size, REACH + k)

            if last:
                pl.when(has(k) & (k != 0))(lambda: result(k).start())
            return carry

        lax.fori_loop(first, stop, step, 0)

    row_a = remote(rowres.at[1], rbuf.at[ZA], S_ROW, R_RES + ZA, (d, from_a))
    row_b = remote(rowres.at[2], rbuf.at[ZB], S_ROW + 1, R_RES + ZB, (d, mate))

    diag(0)

    @pl.when(inner)
    def _():
        z_copy(2, ZB, (d, mate)).wait_recv()
        load_x(ZB, 2)
        for part in range(2):
            z_copy(part, ZB, (d, mate)).wait_recv()
        meet(ZB, 2, mate, 0, q, 0, 4)

    diag(1)
    z_copy(2, ZA, (d, from_a)).wait_recv()
    load_x(ZA, 1)
    z_copy(0, ZA, (d, from_a)).wait_recv()
    meet(ZA, 1, from_a, 0, most, 0, 4)

    pl.when(has(near + sis))(functools.partial(arrived, REACH + near + sis))
    pl.when(has(-near + sis))(functools.partial(arrived, REACH - near + sis))
    lax.fori_loop(4, SLOTS, own_step, 0)
    row_result(0, 0, q)

    @pl.when(inner)
    def _():
        meet(ZB, 2, mate, 0, q, 4, SLOTS)
        row_result(2, 0, q)
        row_b.start()

    meet(ZA, 1, from_a, 0, most, 4, SLOTS)
    z_copy(1, ZA, (d, from_a)).wait_recv()
    meet(ZA, 1, from_a, most, q - most, 0, SLOTS, last=True)
    row_result(1, 0, q)
    row_a.start()

    back = remote(rowres.at[3], rbuf.at[SLOTS + 2], S_ROW + 2, R_RES + SLOTS + 2, (d - 4, 3))

    @pl.when(corner_in)
    def _():
        remote(buf.at[OWN, tail], corner, S_CORNER, R_CORNER, (d - 4, 3)).wait_recv()
        first = buf[OWN, 0:16, :].astype(jnp.float32)[0:1]
        last = corner[0:16, :].astype(jnp.float32)[15:16]
        cos = jnp.sum(first * last, axis=1, keepdims=True)
        here = take_ids(OWN)[:, 0:1]
        there = corner[16:32, 0:q].astype(jnp.float32)[0:1, q - 1 : q]
        top = jnp.broadcast_to(jnp.where(here == there, cos, NO_PAIR), (8, q))
        mass = jnp.exp2(top * LOG2 - LOG2)
        mine = (lanes == 0) & (subs == 0)
        cacc[OWN, 0] = jnp.maximum(cacc[OWN, 0], jnp.where(mine, top, -1.0))
        cacc[OWN, 1] += jnp.where(mine, mass, 0.0)
        theirs = (lanes == q - 1) & (subs == 0)
        rowres[3, 0] = jnp.where(theirs, top, -1.0)
        rowres[3, 1] = jnp.where(theirs, mass, 0.0)
        back.start()

    out_ref[0] = jnp.maximum(rowres[0, 0], cacc[OWN, 0])
    out_ref[1] = rowres[0, 1] + cacc[OWN, 1]

    def add_result(slot):
        remote(rowres.at[0], rbuf.at[slot], S_ROW, R_RES + slot, (sister, z)).wait_recv()
        out_ref[0] = jnp.maximum(out_ref[0], rbuf[slot, 0])
        out_ref[1] += rbuf[slot, 1]

    pl.when(corner_out)(functools.partial(add_result, SLOTS + 2))
    for k in (-3, -2, -1, 1, 2, 3):
        pl.when(has(k))(functools.partial(add_result, REACH + k))
    add_result(ZA)
    pl.when(outer)(functools.partial(add_result, ZB))

    for part in range(3):
        z_copy(part, ZA, (d, to_a)).wait_send()
        pl.when(outer)(z_copy(part, ZB, (d, mate)).wait_send)
    for part in range(2):
        send_near[part].wait_send()
        pl.when(has_far)(send_far[part].wait_send)
        send_sis[part].wait_send()
        pl.when(has_across)(go_across[part].wait_send)
        go_near[part].wait_send()
        pl.when(has_diag)(go_diag[part].wait_send)
    pl.when(corner_out)(send_corner.wait_send)
    for k in (-3, -2, -1, 1, 2, 3):
        pl.when(has(k))(result(k).wait_send)
    row_a.wait_send()
    pl.when(inner)(row_b.wait_send)
    pl.when(corner_in)(back.wait_send)


def finish(both_ref, top_ref, mass_ref):
    top_ref[...] = jnp.max(both_ref[0], axis=0)
    mass_ref[...] = jnp.sum(both_ref[1], axis=0)


def per_device(n, embeds, cluster):
    q, width = embeds.shape
    both = pl.pallas_call(
        functools.partial(kernel, n),
        out_shape=jax.ShapeDtypeStruct((2, 8, q), jnp.float32),
        in_specs=[pl.BlockSpec(memory_space=pltpu.HBM)] * 2,
        out_specs=pl.BlockSpec(memory_space=pltpu.VMEM),
        scratch_shapes=[
            pltpu.VMEM((q, width), jnp.bfloat16),
            pltpu.VMEM((1, q), jnp.int32),
            pltpu.VMEM((SLOTS + 2, q + 16, width), jnp.bfloat16),
            pltpu.VMEM((32, width), jnp.bfloat16),
            pltpu.VMEM((3, q, 128), jnp.float32),
            pltpu.VMEM((3, 2, q, 128), jnp.float32),
            pltpu.VMEM((SLOTS, 2, 8, q), jnp.float32),
            pltpu.VMEM((4, 2, 8, q), jnp.float32),
            pltpu.VMEM((SLOTS + 3, 2, 8, q), jnp.float32),
            pltpu.SemaphoreType.DMA((S_Z + 6,)),
            pltpu.SemaphoreType.DMA((R_Z + 6,)),
            pltpu.SemaphoreType.DMA((2,)),
        ],
        compiler_params=pltpu.CompilerParams(
            collective_id=0, has_side_effects=True, vmem_limit_bytes=63 * 2**20
        ),
        name="dedup",
    )(embeds, cluster.reshape(1, q))
    return jnp.max(both[0], axis=0), jnp.sum(both[1], axis=0)


def solution(mesh):
    return jax.shard_map(
        functools.partial(per_device, mesh.shape["docs"]),
        mesh=mesh,
        in_specs=(P(("docs", "rep"), None), P(("docs", "rep"))),
        out_specs=(P(("docs", "rep")), P(("docs", "rep"))),
        check_vma=False,
    )
```

```python
import functools
import math

import jax
import jax.numpy as jnp
from jax import lax
from jax.experimental import pallas as pl
from jax.experimental.pallas import tpu as pltpu
from jax.sharding import PartitionSpec as P

MESH = pl.DeviceIdType.MESH
dup_scale = 8.0
LOG2 = dup_scale * math.log2(math.e)
NO_PAIR = -100.0
REACH = 3
SLOTS = 2 * REACH + 1
OWN, ZA, ZB = REACH, SLOTS, SLOTS + 1
PARTS = 4
S_CORNER = 6 * PARTS
S_ROW = S_CORNER + 1
S_RES = S_ROW + 3
S_Z = S_RES + SLOTS
R_CORNER = PARTS * SLOTS
R_RES = R_CORNER + 1
R_Z = R_RES + SLOTS + 3


def kernel(
    n,
    e_hbm,
    c_hbm,
    out_ref,
    e_ref,
    c_ref,
    buf,
    corner,
    xids,
    racc,
    cacc,
    rowres,
    rbuf,
    ssem,
    rsem,
    lsem,
):
    q, width = e_ref.shape
    half = q // 2
    d = lax.axis_index("docs")
    z = lax.axis_index("rep")
    odd = lax.rem(d, 2)
    corner_of_four = lax.rem(d, 4)
    low = corner_of_four < 2
    sis = 1 - 2 * odd
    near = jnp.where(low, 2, -2)
    far = 6 * odd - 3
    sister = d + sis
    to_a = jnp.where(z < 2, z + 2, 3 - z)
    from_a = jnp.where(z < 2, 3 - z, z - 2)
    mate = z + 1 - 2 * lax.rem(z, 2)
    inner = (z == 1) | (z == 2)
    outer = (z == 0) | (z == 3)

    def has(k):
        return (d + k >= 0) & (d + k < n)

    corner_in = (z == 0) & has(-4)
    corner_out = (z == 3) & has(4)
    ends = (corner_of_four == 0) | (corner_of_four == 3)

    def remote(src, dst, s, r, dev):
        return pltpu.make_async_remote_copy(
            src_ref=src,
            dst_ref=dst,
            send_sem=ssem.at[s],
            recv_sem=rsem.at[r],
            device_id=dev,
            device_id_type=MESH,
        )

    barrier = pltpu.get_barrier_semaphore()

    def greet(dev):
        pl.semaphore_signal(barrier, inc=1, device_id=dev, device_id_type=MESH)

    load_e = pltpu.make_async_copy(e_hbm, e_ref, lsem.at[0])
    load_c = pltpu.make_async_copy(c_hbm, c_ref, lsem.at[1])
    load_e.start()
    load_c.start()
    total = jnp.int32(3)
    for k in (-3, -2, -1, 1, 2, 3):
        pl.when(has(k))(functools.partial(greet, (d + k, z)))
        total = total + has(k).astype(jnp.int32)
    for k in (-4, 4):
        pl.when(has(k) & ends)(functools.partial(greet, (d + k, z)))
        total = total + (has(k) & ends).astype(jnp.int32)
    greet((d, to_a))
    greet((d, from_a))
    greet((d, mate))
    pl.when(corner_in)(functools.partial(greet, (d - 4, 3)))
    pl.when(corner_out)(functools.partial(greet, (d + 4, 0)))
    total = total + corner_in.astype(jnp.int32) + corner_out.astype(jnp.int32)

    id_rows = pl.ds(q, 16)

    def z_copy(part, slot, dev):
        first = 3 * (slot - ZA)
        if part == 2:
            view = (id_rows, pl.ds(0, q))
        else:
            view = (pl.ds(part * half, half),)
        return remote(
            buf.at[(OWN,) + view],
            buf.at[(slot,) + view],
            S_Z + first + part,
            R_Z + first + part,
            dev,
        )

    def send_z(part):
        pl.when(outer)(z_copy(part, ZB, (d, mate)).start)
        z_copy(part, ZA, (d, to_a)).start()

    def pieces(slot, to, s, dev):
        size = q // PARTS
        views = [pl.ds(part * size, size) for part in range(PARTS - 1)]
        views.append(pl.ds(q - size, size + 16))
        return [
            remote(buf.at[slot, view], buf.at[to, view], PARTS * s + part, PARTS * to + part, dev)
            for part, view in enumerate(views)
        ]

    send_near = pieces(OWN, REACH - near, 0, (d + near, z))
    send_far = pieces(OWN, REACH - far, 1, (d + far, z))
    send_sis = pieces(OWN, REACH - sis, 2, (sister, z))
    has_far = has(far)
    tail = pl.ds(q - 16, 32)
    send_corner = remote(buf.at[OWN, tail], corner, S_CORNER, R_CORNER, (d + 4, 0))

    load_c.wait()
    ids = c_ref[...].astype(jnp.float32)
    buf[OWN, q : q + 16, :] = jnp.zeros((16, width), jnp.bfloat16)
    buf[OWN, q : q + 16, 0:q] = jnp.broadcast_to(ids, (16, q)).astype(jnp.bfloat16)
    load_e.wait()
    for part in range(2):
        rows = pl.ds(part * half, half)
        x = e_ref[rows, :].astype(jnp.float32)
        scale = lax.rsqrt(jnp.mean(x * x, axis=1, keepdims=True) + 1e-06)
        buf[OWN, rows, :] = (x * scale * width ** (-0.5)).astype(jnp.bfloat16)
        if part == 0:
            pl.semaphore_wait(barrier, total)
        ready = range(part * PARTS // 2, (part + 1) * PARTS // 2)
        for piece in ready:
            pl.when(has_far)(send_far[piece].start)
            send_near[piece].start()
        send_z(part)
        for piece in ready:
            send_sis[piece].start()
        if part == 0:
            send_z(2)
    pl.when(corner_out)(send_corner.start)

    lanes = lax.broadcasted_iota(jnp.int32, (8, q), 1)
    subs = lax.broadcasted_iota(jnp.int32, (8, q), 0)

    def take_ids(slot):
        return buf[slot, q : q + 16, 0:q].astype(jnp.float32)[0:1]

    def load_x(slot, xi):
        xids[xi] = jnp.broadcast_to(take_ids(slot), (128, q)).T

    def tile(xslot, xi, start, size, slot, diagonal=False):
        rows = pl.ds(start, size)
        scores = lax.dot_general(
            buf[xslot, rows, :],
            buf[slot, 0:q, :],
            (((1,), (1,)), ((), ())),
            preferred_element_type=jnp.float32,
        )
        yid = take_ids(slot)
        xid = xids[xi, rows, :]
        tops, masses = [], []
        for lo in range(0, q, 128):
            mask = xid == yid[:, lo : lo + 128]
            if diagonal:
                i = lax.broadcasted_iota(jnp.int32, (size, 128), 0)
                j = lax.broadcasted_iota(jnp.int32, (size, 128), 1) + lo
                mask = mask & (i != j)
            top = jnp.where(mask, scores[:, lo : lo + 128], NO_PAIR)
            mass = jnp.exp2(top * LOG2 - LOG2)
            cols = pl.ds(lo, 128)
            cacc[slot, 0, :, cols] = jnp.maximum(
                cacc[slot, 0, :, cols], jnp.max(top.reshape(size // 8, 8, 128), axis=0)
            )
            cacc[slot, 1, :, cols] += jnp.sum(mass.reshape(size // 8, 8, 128), axis=0)
            tops.append(top)
            masses.append(mass)
        if not diagonal:
            racc[xi, 0, rows, :] = jnp.maximum(
                racc[xi, 0, rows, :], functools.reduce(jnp.maximum, tops)
            )
            racc[xi, 1, rows, :] += functools.reduce(jnp.add, masses)

    def row_result(xi, start, size):
        rows = pl.ds(start, size)
        rowres[xi, 0, :, rows] = jnp.max(racc[xi, 0, rows, :].T.reshape(16, 8, size), axis=0)
        rowres[xi, 1, :, rows] = jnp.sum(racc[xi, 1, rows, :].T.reshape(16, 8, size), axis=0)

    cacc[:, 0] = jnp.full((SLOTS, 8, q), -1.0, jnp.float32)
    cacc[:, 1] = jnp.zeros((SLOTS, 8, q), jnp.float32)

    racc[:, 0] = jnp.full((3, q, 128), -1.0, jnp.float32)
    racc[:, 1] = jnp.zeros((3, q, 128), jnp.float32)
    load_x(OWN, 0)
    tile(OWN, 0, 0, q, OWN, diagonal=True)

    def arrived(slot, parts=range(PARTS)):
        copies = pieces(OWN, slot, 0, (sister, z))
        for part in parts:
            copies[part].wait_recv()

    across = jnp.where(low, 4 - 3 * odd, -1 - 3 * odd)
    across_from = jnp.where(low, 2 + odd, -3 + odd)
    has_across = has(across) & has(across_from)

    def go_on(slot, s, by):
        return pieces(slot, slot - by, s, (d + by, z))

    go_across = go_on(REACH + across_from, 3, across)
    go_near = go_on(REACH + near, 4, sis)
    go_diag = go_on(REACH - near, 5, sis)
    has_diag = has(-near)

    for part in range(PARTS):
        pl.when(has_far)(functools.partial(arrived, REACH + far, (part,)))
        pl.when(has_across & jnp.logical_not(ends))(go_across[part].start)
        arrived(REACH + near, (part,))
        pl.when(has_across & ends)(go_across[part].start)
        go_near[part].start()
    arrived(REACH + sis)

    order = (0, sis, near, far, near + sis, -near, -near + sis)

    def nth(i):
        k = jnp.int32(0)
        for j in range(1, SLOTS):
            k = jnp.where(i == j, order[j], k)
        return k

    def own_step(i, carry):
        k = nth(i)

        @pl.when((k > 0) & has(k))
        def _():
            tile(OWN, 0, 0, q, REACH + k)

        return carry

    lax.fori_loop(1, 4, own_step, 0)

    def diag(part):
        @pl.when(has_diag)
        def _():
            arrived(REACH - near, (part,))
            go_diag[part].start()

    def result(k):
        return remote(
            cacc.at[REACH + k],
            rbuf.at[REACH - k],
            S_RES + REACH + k,
            R_RES + REACH - k,
            (d + k, z),
        )

    def meet(slot, xi, xz, start, size, first, stop, last=False):
        def step(i, carry):
            k = nth(i)
            apart = ((k == REACH) & (xz < z - 1)) | ((k == -REACH) & (z < xz - 1))

            @pl.when(has(k) & jnp.logical_not(apart))
            def _():
                tile(slot, xi, start, size, REACH + k)

            if last:
                pl.when(has(k) & (k != 0))(lambda: result(k).start())
            return carry

        lax.fori_loop(first, stop, step, 0)

    row_a = remote(rowres.at[1], rbuf.at[ZA], S_ROW, R_RES + ZA, (d, from_a))
    row_b = remote(rowres.at[2], rbuf.at[ZB], S_ROW + 1, R_RES + ZB, (d, mate))

    for part in range(PARTS // 2):
        diag(part)

    @pl.when(inner)
    def _():
        z_copy(2, ZB, (d, mate)).wait_recv()
        load_x(ZB, 2)
        for part in range(2):
            z_copy(part, ZB, (d, mate)).wait_recv()
        meet(ZB, 2, mate, 0, q, 0, 4)

    for part in range(PARTS // 2, PARTS):
        diag(part)
    pl.when(has(near + sis))(functools.partial(arrived, REACH + near + sis))
    pl.when(has(-near + sis))(functools.partial(arrived, REACH - near + sis))
    lax.fori_loop(4, SLOTS, own_step, 0)
    row_result(0, 0, q)

    @pl.when(inner)
    def _():
        meet(ZB, 2, mate, 0, q, 4, SLOTS)
        row_result(2, 0, q)
        row_b.start()

    z_copy(2, ZA, (d, from_a)).wait_recv()
    load_x(ZA, 1)
    z_copy(0, ZA, (d, from_a)).wait_recv()
    meet(ZA, 1, from_a, 0, half, 0, SLOTS)
    row_result(1, 0, half)
    z_copy(1, ZA, (d, from_a)).wait_recv()
    meet(ZA, 1, from_a, half, half, 0, SLOTS, last=True)
    row_result(1, half, half)
    row_a.start()

    back = remote(rowres.at[3], rbuf.at[SLOTS + 2], S_ROW + 2, R_RES + SLOTS + 2, (d - 4, 3))

    @pl.when(corner_in)
    def _():
        remote(buf.at[OWN, tail], corner, S_CORNER, R_CORNER, (d - 4, 3)).wait_recv()
        first = buf[OWN, 0:16, :].astype(jnp.float32)[0:1]
        last = corner[0:16, :].astype(jnp.float32)[15:16]
        cos = jnp.sum(first * last, axis=1, keepdims=True)
        here = take_ids(OWN)[:, 0:1]
        there = corner[16:32, 0:q].astype(jnp.float32)[0:1, q - 1 : q]
        top = jnp.broadcast_to(jnp.where(here == there, cos, NO_PAIR), (8, q))
        mass = jnp.exp2(top * LOG2 - LOG2)
        mine = (lanes == 0) & (subs == 0)
        cacc[OWN, 0] = jnp.maximum(cacc[OWN, 0], jnp.where(mine, top, -1.0))
        cacc[OWN, 1] += jnp.where(mine, mass, 0.0)
        theirs = (lanes == q - 1) & (subs == 0)
        rowres[3, 0] = jnp.where(theirs, top, -1.0)
        rowres[3, 1] = jnp.where(theirs, mass, 0.0)
        back.start()

    out_ref[0] = jnp.maximum(rowres[0, 0], cacc[OWN, 0])
    out_ref[1] = rowres[0, 1] + cacc[OWN, 1]

    def add_result(slot):
        remote(rowres.at[0], rbuf.at[slot], S_ROW, R_RES + slot, (sister, z)).wait_recv()
        out_ref[0] = jnp.maximum(out_ref[0], rbuf[slot, 0])
        out_ref[1] += rbuf[slot, 1]

    pl.when(corner_out)(functools.partial(add_result, SLOTS + 2))
    for k in (-3, -2, -1, 1, 2, 3):
        pl.when(has(k))(functools.partial(add_result, REACH + k))
    add_result(ZA)
    pl.when(outer)(functools.partial(add_result, ZB))

    for part in range(3):
        z_copy(part, ZA, (d, to_a)).wait_send()
        pl.when(outer)(z_copy(part, ZB, (d, mate)).wait_send)
    for part in range(PARTS):
        send_near[part].wait_send()
        pl.when(has_far)(send_far[part].wait_send)
        send_sis[part].wait_send()
        pl.when(has_across)(go_across[part].wait_send)
        go_near[part].wait_send()
        pl.when(has_diag)(go_diag[part].wait_send)
    pl.when(corner_out)(send_corner.wait_send)
    for k in (-3, -2, -1, 1, 2, 3):
        pl.when(has(k))(result(k).wait_send)
    row_a.wait_send()
    pl.when(inner)(row_b.wait_send)
    pl.when(corner_in)(back.wait_send)


def finish(both_ref, top_ref, mass_ref):
    top_ref[...] = jnp.max(both_ref[0], axis=0)
    mass_ref[...] = jnp.sum(both_ref[1], axis=0)


def per_device(n, embeds, cluster):
    q, width = embeds.shape
    both = pl.pallas_call(
        functools.partial(kernel, n),
        out_shape=jax.ShapeDtypeStruct((2, 8, q), jnp.float32),
        in_specs=[pl.BlockSpec(memory_space=pltpu.HBM)] * 2,
        out_specs=pl.BlockSpec(memory_space=pltpu.VMEM),
        scratch_shapes=[
            pltpu.VMEM((q, width), jnp.bfloat16),
            pltpu.VMEM((1, q), jnp.int32),
            pltpu.VMEM((SLOTS + 2, q + 16, width), jnp.bfloat16),
            pltpu.VMEM((32, width), jnp.bfloat16),
            pltpu.VMEM((3, q, 128), jnp.float32),
            pltpu.VMEM((3, 2, q, 128), jnp.float32),
            pltpu.VMEM((SLOTS, 2, 8, q), jnp.float32),
            pltpu.VMEM((4, 2, 8, q), jnp.float32),
            pltpu.VMEM((SLOTS + 3, 2, 8, q), jnp.float32),
            pltpu.SemaphoreType.DMA((S_Z + 6,)),
            pltpu.SemaphoreType.DMA((R_Z + 6,)),
            pltpu.SemaphoreType.DMA((2,)),
        ],
        compiler_params=pltpu.CompilerParams(
            collective_id=0, has_side_effects=True, vmem_limit_bytes=63 * 2**20
        ),
        name="dedup",
    )(embeds, cluster.reshape(1, q))
    return pl.pallas_call(
        finish,
        out_shape=(jax.ShapeDtypeStruct((q,), jnp.float32),) * 2,
        in_specs=[pl.BlockSpec(memory_space=pltpu.VMEM)],
        out_specs=(pl.BlockSpec(memory_space=pltpu.VMEM),) * 2,
        name="finish",
    )(both)


def solution(mesh):
    return jax.shard_map(
        functools.partial(per_device, mesh.shape["docs"]),
        mesh=mesh,
        in_specs=(P(("docs", "rep"), None), P(("docs", "rep"))),
        out_specs=(P(("docs", "rep")), P(("docs", "rep"))),
        check_vma=False,
    )
```

```python
import functools
import math

import jax
import jax.numpy as jnp
from jax import lax
from jax.experimental import pallas as pl
from jax.experimental.pallas import tpu as pltpu
from jax.sharding import PartitionSpec as P

MESH = pl.DeviceIdType.MESH
dup_scale = 8.0
LOG2 = dup_scale * math.log2(math.e)
NO_PAIR = -100.0
REACH = 3
SLOTS = 2 * REACH + 1
OWN, ZA, ZB = REACH, SLOTS, SLOTS + 1
S_CORNER = 12
S_ROW = S_CORNER + 1
S_RES = S_ROW + 3
S_Z = S_RES + SLOTS
R_CORNER = 2 * SLOTS
R_RES = R_CORNER + 1
R_Z = R_RES + SLOTS + 3


def kernel(
    n,
    e_hbm,
    c_hbm,
    out_ref,
    e_ref,
    c_ref,
    buf,
    corner,
    xids,
    racc,
    cacc,
    rowres,
    rbuf,
    ssem,
    rsem,
    lsem,
):
    q, width = e_ref.shape
    half = q // 2
    d = lax.axis_index("docs")
    z = lax.axis_index("rep")
    odd = lax.rem(d, 2)
    corner_of_four = lax.rem(d, 4)
    low = corner_of_four < 2
    sis = 1 - 2 * odd
    near = jnp.where(low, 2, -2)
    far = 6 * odd - 3
    sister = d + sis
    to_a = jnp.where(z < 2, z + 2, 3 - z)
    from_a = jnp.where(z < 2, 3 - z, z - 2)
    mate = z + 1 - 2 * lax.rem(z, 2)
    inner = (z == 1) | (z == 2)
    outer = (z == 0) | (z == 3)

    def has(k):
        return (d + k >= 0) & (d + k < n)

    corner_in = (z == 0) & has(-4)
    corner_out = (z == 3) & has(4)
    ends = (corner_of_four == 0) | (corner_of_four == 3)

    def remote(src, dst, s, r, dev):
        return pltpu.make_async_remote_copy(
            src_ref=src,
            dst_ref=dst,
            send_sem=ssem.at[s],
            recv_sem=rsem.at[r],
            device_id=dev,
            device_id_type=MESH,
        )

    barrier = pltpu.get_barrier_semaphore()

    def greet(dev):
        pl.semaphore_signal(barrier, inc=1, device_id=dev, device_id_type=MESH)

    bands = [pl.ds(i * q // 4, q // 4) for i in range(4)]
    load_e = [
        pltpu.make_async_copy(e_hbm.at[rows], e_ref.at[rows], lsem.at[i])
        for i, rows in enumerate(bands)
    ]
    load_c = pltpu.make_async_copy(c_hbm, c_ref, lsem.at[4])
    load_e[0].start()
    load_c.start()
    for load in load_e[1:]:
        load.start()
    total = jnp.int32(3)
    for k in (-3, -2, -1, 1, 2, 3):
        pl.when(has(k))(functools.partial(greet, (d + k, z)))
        total = total + has(k).astype(jnp.int32)
    for k in (-4, 4):
        pl.when(has(k) & ends)(functools.partial(greet, (d + k, z)))
        total = total + (has(k) & ends).astype(jnp.int32)
    greet((d, to_a))
    greet((d, from_a))
    greet((d, mate))
    pl.when(corner_in)(functools.partial(greet, (d - 4, 3)))
    pl.when(corner_out)(functools.partial(greet, (d + 4, 0)))
    total = total + corner_in.astype(jnp.int32) + corner_out.astype(jnp.int32)

    id_rows = pl.ds(q, 16)

    def z_copy(part, slot, dev):
        first = 3 * (slot - ZA)
        if part == 2:
            view = (id_rows, pl.ds(0, q))
        else:
            view = (pl.ds(part * half, half),)
        return remote(
            buf.at[(OWN,) + view],
            buf.at[(slot,) + view],
            S_Z + first + part,
            R_Z + first + part,
            dev,
        )

    def send_z(part):
        pl.when(outer)(z_copy(part, ZB, (d, mate)).start)
        z_copy(part, ZA, (d, to_a)).start()

    def halves(slot, to, s, dev):
        return [
            remote(buf.at[slot, view], buf.at[to, view], 2 * s + part, 2 * to + part, dev)
            for part, view in enumerate((pl.ds(0, half), pl.ds(half, half + 16)))
        ]

    send_near = halves(OWN, REACH - near, 0, (d + near, z))
    send_far = halves(OWN, REACH - far, 1, (d + far, z))
    send_sis = halves(OWN, REACH - sis, 2, (sister, z))
    has_far = has(far)
    tail = pl.ds(q - 16, 32)
    send_corner = remote(buf.at[OWN, tail], corner, S_CORNER, R_CORNER, (d + 4, 0))

    for part in range(2):
        for i in (2 * part, 2 * part + 1):
            load_e[i].wait()
            x = e_ref[bands[i], :].astype(jnp.float32)
            scale = lax.rsqrt(jnp.mean(x * x, axis=1, keepdims=True) + 1e-06)
            buf[OWN, bands[i], :] = (x * scale * width ** (-0.5)).astype(jnp.bfloat16)
        if part == 0:
            pl.semaphore_wait(barrier, total)
        pl.when(has_far)(send_far[part].start)
        send_near[part].start()
        send_z(part)
        send_sis[part].start()
        if part == 0:
            load_c.wait()
            ids = c_ref[...].astype(jnp.float32)
            buf[OWN, q : q + 16, :] = jnp.zeros((16, width), jnp.bfloat16)
            buf[OWN, q : q + 16, 0:q] = jnp.broadcast_to(ids, (16, q)).astype(jnp.bfloat16)
            send_z(2)
    pl.when(corner_out)(send_corner.start)

    lanes = lax.broadcasted_iota(jnp.int32, (8, q), 1)
    subs = lax.broadcasted_iota(jnp.int32, (8, q), 0)

    def take_ids(slot):
        return buf[slot, q : q + 16, 0:q].astype(jnp.float32)[0:1]

    def load_x(slot, xi):
        xids[xi] = jnp.broadcast_to(take_ids(slot), (128, q)).T

    def tile(xslot, xi, start, size, slot, diagonal=False):
        rows = pl.ds(start, size)
        scores = lax.dot_general(
            buf[xslot, rows, :],
            buf[slot, 0:q, :],
            (((1,), (1,)), ((), ())),
            preferred_element_type=jnp.float32,
        )
        yid = take_ids(slot)
        xid = xids[xi, rows, :]
        tops, masses = [], []
        for lo in range(0, q, 128):
            mask = xid == yid[:, lo : lo + 128]
            if diagonal:
                i = lax.broadcasted_iota(jnp.int32, (size, 128), 0)
                j = lax.broadcasted_iota(jnp.int32, (size, 128), 1) + lo
                mask = mask & (i != j)
            top = jnp.where(mask, scores[:, lo : lo + 128], NO_PAIR)
            mass = jnp.exp2(top * LOG2 - LOG2)
            cols = pl.ds(lo, 128)
            cacc[slot, 0, :, cols] = jnp.maximum(
                cacc[slot, 0, :, cols], jnp.max(top.reshape(size // 8, 8, 128), axis=0)
            )
            cacc[slot, 1, :, cols] += jnp.sum(mass.reshape(size // 8, 8, 128), axis=0)
            tops.append(top)
            masses.append(mass)
        if not diagonal:
            racc[xi, 0, rows, :] = jnp.maximum(
                racc[xi, 0, rows, :], functools.reduce(jnp.maximum, tops)
            )
            racc[xi, 1, rows, :] += functools.reduce(jnp.add, masses)

    def row_result(xi, start, size):
        rows = pl.ds(start, size)
        rowres[xi, 0, :, rows] = jnp.max(racc[xi, 0, rows, :].T.reshape(16, 8, size), axis=0)
        rowres[xi, 1, :, rows] = jnp.sum(racc[xi, 1, rows, :].T.reshape(16, 8, size), axis=0)

    cacc[:, 0] = jnp.full((SLOTS, 8, q), -1.0, jnp.float32)
    cacc[:, 1] = jnp.zeros((SLOTS, 8, q), jnp.float32)

    racc[:, 0] = jnp.full((3, q, 128), -1.0, jnp.float32)
    racc[:, 1] = jnp.zeros((3, q, 128), jnp.float32)
    load_x(OWN, 0)
    tile(OWN, 0, 0, q, OWN, diagonal=True)

    def arrived(slot, parts=(0, 1)):
        copies = halves(OWN, slot, 0, (sister, z))
        for part in parts:
            copies[part].wait_recv()

    across = jnp.where(low, 4 - 3 * odd, -1 - 3 * odd)
    across_from = jnp.where(low, 2 + odd, -3 + odd)
    has_across = has(across) & has(across_from)

    def go_on(slot, s, by):
        return halves(slot, slot - by, s, (d + by, z))

    go_across = go_on(REACH + across_from, 3, across)
    go_near = go_on(REACH + near, 4, sis)
    go_diag = go_on(REACH - near, 5, sis)
    has_diag = has(-near)

    for part in range(2):
        pl.when(has_far)(functools.partial(arrived, REACH + far, (part,)))
        pl.when(has_across & jnp.logical_not(ends))(go_across[part].start)
        arrived(REACH + near, (part,))
        pl.when(has_across & ends)(go_across[part].start)
        go_near[part].start()
    arrived(REACH + sis)

    order = (0, sis, near, far, near + sis, -near, -near + sis)

    def nth(i):
        k = jnp.int32(0)
        for j in range(1, SLOTS):
            k = jnp.where(i == j, order[j], k)
        return k

    def own_step(i, carry):
        k = nth(i)

        @pl.when((k > 0) & has(k))
        def _():
            tile(OWN, 0, 0, q, REACH + k)

        return carry

    lax.fori_loop(1, 4, own_step, 0)

    def diag(part):
        @pl.when(has_diag)
        def _():
            arrived(REACH - near, (part,))
            go_diag[part].start()

    def result(k):
        return remote(
            cacc.at[REACH + k],
            rbuf.at[REACH - k],
            S_RES + REACH + k,
            R_RES + REACH - k,
            (d + k, z),
        )

    def meet(slot, xi, xz, start, size, first, stop, last=False):
        def step(i, carry):
            k = nth(i)
            apart = ((k == REACH) & (xz < z - 1)) | ((k == -REACH) & (z < xz - 1))

            @pl.when(has(k) & jnp.logical_not(apart))
            def _():
                tile(slot, xi, start, size, REACH + k)

            if last:
                pl.when(has(k) & (k != 0))(lambda: result(k).start())
            return carry

        lax.fori_loop(first, stop, step, 0)

    row_a = remote(rowres.at[1], rbuf.at[ZA], S_ROW, R_RES + ZA, (d, from_a))
    row_b = remote(rowres.at[2], rbuf.at[ZB], S_ROW + 1, R_RES + ZB, (d, mate))

    diag(0)

    @pl.when(inner)
    def _():
        z_copy(2, ZB, (d, mate)).wait_recv()
        load_x(ZB, 2)
        for part in range(2):
            z_copy(part, ZB, (d, mate)).wait_recv()
        meet(ZB, 2, mate, 0, q, 0, 4)

    diag(1)
    z_copy(2, ZA, (d, from_a)).wait_recv()
    load_x(ZA, 1)
    z_copy(0, ZA, (d, from_a)).wait_recv()
    meet(ZA, 1, from_a, 0, half, 0, 4)

    pl.when(has(near + sis))(functools.partial(arrived, REACH + near + sis))
    pl.when(has(-near + sis))(functools.partial(arrived, REACH - near + sis))
    lax.fori_loop(4, SLOTS, own_step, 0)
    row_result(0, 0, q)

    @pl.when(inner)
    def _():
        meet(ZB, 2, mate, 0, q, 4, SLOTS)
        row_result(2, 0, q)
        row_b.start()

    meet(ZA, 1, from_a, 0, half, 4, SLOTS)
    row_result(1, 0, half)
    z_copy(1, ZA, (d, from_a)).wait_recv()
    meet(ZA, 1, from_a, half, half, 0, SLOTS, last=True)
    row_result(1, half, half)
    row_a.start()

    back = remote(rowres.at[3], rbuf.at[SLOTS + 2], S_ROW + 2, R_RES + SLOTS + 2, (d - 4, 3))

    @pl.when(corner_in)
    def _():
        remote(buf.at[OWN, tail], corner, S_CORNER, R_CORNER, (d - 4, 3)).wait_recv()
        first = buf[OWN, 0:16, :].astype(jnp.float32)[0:1]
        last = corner[0:16, :].astype(jnp.float32)[15:16]
        cos = jnp.sum(first * last, axis=1, keepdims=True)
        here = take_ids(OWN)[:, 0:1]
        there = corner[16:32, 0:q].astype(jnp.float32)[0:1, q - 1 : q]
        top = jnp.broadcast_to(jnp.where(here == there, cos, NO_PAIR), (8, q))
        mass = jnp.exp2(top * LOG2 - LOG2)
        mine = (lanes == 0) & (subs == 0)
        cacc[OWN, 0] = jnp.maximum(cacc[OWN, 0], jnp.where(mine, top, -1.0))
        cacc[OWN, 1] += jnp.where(mine, mass, 0.0)
        theirs = (lanes == q - 1) & (subs == 0)
        rowres[3, 0] = jnp.where(theirs, top, -1.0)
        rowres[3, 1] = jnp.where(theirs, mass, 0.0)
        back.start()

    out_ref[0] = jnp.maximum(rowres[0, 0], cacc[OWN, 0])
    out_ref[1] = rowres[0, 1] + cacc[OWN, 1]

    def add_result(slot):
        remote(rowres.at[0], rbuf.at[slot], S_ROW, R_RES + slot, (sister, z)).wait_recv()
        out_ref[0] = jnp.maximum(out_ref[0], rbuf[slot, 0])
        out_ref[1] += rbuf[slot, 1]

    pl.when(corner_out)(functools.partial(add_result, SLOTS + 2))
    for k in (-3, -2, -1, 1, 2, 3):
        pl.when(has(k))(functools.partial(add_result, REACH + k))
    add_result(ZA)
    pl.when(outer)(functools.partial(add_result, ZB))

    for part in range(3):
        z_copy(part, ZA, (d, to_a)).wait_send()
        pl.when(outer)(z_copy(part, ZB, (d, mate)).wait_send)
    for part in range(2):
        send_near[part].wait_send()
        pl.when(has_far)(send_far[part].wait_send)
        send_sis[part].wait_send()
        pl.when(has_across)(go_across[part].wait_send)
        go_near[part].wait_send()
        pl.when(has_diag)(go_diag[part].wait_send)
    pl.when(corner_out)(send_corner.wait_send)
    for k in (-3, -2, -1, 1, 2, 3):
        pl.when(has(k))(result(k).wait_send)
    row_a.wait_send()
    pl.when(inner)(row_b.wait_send)
    pl.when(corner_in)(back.wait_send)


def finish(both_ref, top_ref, mass_ref):
    top_ref[...] = jnp.max(both_ref[0], axis=0)
    mass_ref[...] = jnp.sum(both_ref[1], axis=0)


def per_device(n, embeds, cluster):
    q, width = embeds.shape
    both = pl.pallas_call(
        functools.partial(kernel, n),
        out_shape=jax.ShapeDtypeStruct((2, 8, q), jnp.float32),
        in_specs=[pl.BlockSpec(memory_space=pltpu.HBM)] * 2,
        out_specs=pl.BlockSpec(memory_space=pltpu.VMEM),
        scratch_shapes=[
            pltpu.VMEM((q, width), jnp.bfloat16),
            pltpu.VMEM((1, q), jnp.int32),
            pltpu.VMEM((SLOTS + 2, q + 16, width), jnp.bfloat16),
            pltpu.VMEM((32, width), jnp.bfloat16),
            pltpu.VMEM((3, q, 128), jnp.float32),
            pltpu.VMEM((3, 2, q, 128), jnp.float32),
            pltpu.VMEM((SLOTS, 2, 8, q), jnp.float32),
            pltpu.VMEM((4, 2, 8, q), jnp.float32),
            pltpu.VMEM((SLOTS + 3, 2, 8, q), jnp.float32),
            pltpu.SemaphoreType.DMA((S_Z + 6,)),
            pltpu.SemaphoreType.DMA((R_Z + 6,)),
            pltpu.SemaphoreType.DMA((5,)),
        ],
        compiler_params=pltpu.CompilerParams(
            collective_id=0, has_side_effects=True, vmem_limit_bytes=63 * 2**20
        ),
        name="dedup",
    )(embeds, cluster.reshape(1, q))
    return pl.pallas_call(
        finish,
        out_shape=(jax.ShapeDtypeStruct((q,), jnp.float32),) * 2,
        in_specs=[pl.BlockSpec(memory_space=pltpu.VMEM)],
        out_specs=(pl.BlockSpec(memory_space=pltpu.VMEM),) * 2,
        name="finish",
    )(both)


def solution(mesh):
    return jax.shard_map(
        functools.partial(per_device, mesh.shape["docs"]),
        mesh=mesh,
        in_specs=(P(("docs", "rep"), None), P(("docs", "rep"))),
        out_specs=(P(("docs", "rep")), P(("docs", "rep"))),
        check_vma=False,
    )
```

```python
import functools
import math

import jax
import jax.numpy as jnp
from jax import lax
from jax.experimental import pallas as pl
from jax.experimental.pallas import tpu as pltpu
from jax.sharding import PartitionSpec as P

MESH = pl.DeviceIdType.MESH
dup_scale = 8.0
LOG2 = dup_scale * math.log2(math.e)
NO_PAIR = -100.0
REACH = 3
SLOTS = 2 * REACH + 1
OWN, ZA, ZB = REACH, SLOTS, SLOTS + 1
S_CORNER = 12
S_ROW = S_CORNER + 1
S_RES = S_ROW + 3
S_Z = S_RES + SLOTS
R_CORNER = 2 * SLOTS
R_RES = R_CORNER + 1
R_Z = R_RES + SLOTS + 3


def kernel(
    n,
    e_hbm,
    c_hbm,
    out_ref,
    e_ref,
    c_ref,
    buf,
    corner,
    xids,
    racc,
    cacc,
    rowres,
    rbuf,
    ssem,
    rsem,
    lsem,
):
    q, width = e_ref.shape
    half = q // 2
    d = lax.axis_index("docs")
    z = lax.axis_index("rep")
    odd = lax.rem(d, 2)
    corner_of_four = lax.rem(d, 4)
    low = corner_of_four < 2
    sis = 1 - 2 * odd
    near = jnp.where(low, 2, -2)
    far = 6 * odd - 3
    sister = d + sis
    to_a = jnp.where(z < 2, z + 2, 3 - z)
    from_a = jnp.where(z < 2, 3 - z, z - 2)
    mate = z + 1 - 2 * lax.rem(z, 2)
    inner = (z == 1) | (z == 2)
    outer = (z == 0) | (z == 3)

    def has(k):
        return (d + k >= 0) & (d + k < n)

    corner_in = (z == 0) & has(-4)
    corner_out = (z == 3) & has(4)
    ends = (corner_of_four == 0) | (corner_of_four == 3)

    def remote(src, dst, s, r, dev):
        return pltpu.make_async_remote_copy(
            src_ref=src,
            dst_ref=dst,
            send_sem=ssem.at[s],
            recv_sem=rsem.at[r],
            device_id=dev,
            device_id_type=MESH,
        )

    barrier = pltpu.get_barrier_semaphore()

    def greet(dev):
        pl.semaphore_signal(barrier, inc=1, device_id=dev, device_id_type=MESH)

    load_e = pltpu.make_async_copy(e_hbm, e_ref, lsem.at[0])
    load_c = pltpu.make_async_copy(c_hbm, c_ref, lsem.at[1])
    load_e.start()
    load_c.start()
    total = jnp.int32(3)
    for k in (-3, -2, -1, 1, 2, 3):
        pl.when(has(k))(functools.partial(greet, (d + k, z)))
        total = total + has(k).astype(jnp.int32)
    for k in (-4, 4):
        pl.when(has(k) & ends)(functools.partial(greet, (d + k, z)))
        total = total + (has(k) & ends).astype(jnp.int32)
    greet((d, to_a))
    greet((d, from_a))
    greet((d, mate))
    pl.when(corner_in)(functools.partial(greet, (d - 4, 3)))
    pl.when(corner_out)(functools.partial(greet, (d + 4, 0)))
    total = total + corner_in.astype(jnp.int32) + corner_out.astype(jnp.int32)

    id_rows = pl.ds(q, 16)

    def z_copy(part, slot, dev):
        first = 3 * (slot - ZA)
        if part == 2:
            view = (id_rows, pl.ds(0, q))
        else:
            view = (pl.ds(part * half, half),)
        return remote(
            buf.at[(OWN,) + view],
            buf.at[(slot,) + view],
            S_Z + first + part,
            R_Z + first + part,
            dev,
        )

    def send_z(part):
        pl.when(outer)(z_copy(part, ZB, (d, mate)).start)
        z_copy(part, ZA, (d, to_a)).start()

    def halves(slot, to, s, dev):
        return [
            remote(buf.at[slot, view], buf.at[to, view], 2 * s + part, 2 * to + part, dev)
            for part, view in enumerate((pl.ds(0, half), pl.ds(half, half + 16)))
        ]

    send_near = halves(OWN, REACH - near, 0, (d + near, z))
    send_far = halves(OWN, REACH - far, 1, (d + far, z))
    send_sis = halves(OWN, REACH - sis, 2, (sister, z))
    has_far = has(far)
    tail = pl.ds(q - 16, 32)
    send_corner = remote(buf.at[OWN, tail], corner, S_CORNER, R_CORNER, (d + 4, 0))

    load_c.wait()
    ids = c_ref[...].astype(jnp.float32)
    buf[OWN, q : q + 16, :] = jnp.zeros((16, width), jnp.bfloat16)
    buf[OWN, q : q + 16, 0:q] = jnp.broadcast_to(ids, (16, q)).astype(jnp.bfloat16)
    load_e.wait()
    for part in range(2):
        rows = pl.ds(part * half, half)
        x = e_ref[rows, :].astype(jnp.float32)
        scale = lax.rsqrt(jnp.mean(x * x, axis=1, keepdims=True) + 1e-06)
        buf[OWN, rows, :] = (x * scale * width ** (-0.5)).astype(jnp.bfloat16)
        if part == 0:
            pl.semaphore_wait(barrier, total)
        pl.when(has_far)(send_far[part].start)
        send_near[part].start()
        send_z(part)
        send_sis[part].start()
        if part == 0:
            send_z(2)
    pl.when(corner_out)(send_corner.start)

    lanes = lax.broadcasted_iota(jnp.int32, (8, q), 1)
    subs = lax.broadcasted_iota(jnp.int32, (8, q), 0)

    def take_ids(slot):
        return buf[slot, q : q + 16, 0:q].astype(jnp.float32)[0:1]

    def load_x(slot, xi):
        xids[xi] = jnp.broadcast_to(take_ids(slot), (128, q)).T

    def tile(xslot, xi, start, size, slot, diagonal=False):
        rows = pl.ds(start, size)
        scores = lax.dot_general(
            buf[xslot, rows, :],
            buf[slot, 0:q, :],
            (((1,), (1,)), ((), ())),
            preferred_element_type=jnp.float32,
        )
        yid = take_ids(slot)
        xid = xids[xi, rows, :]
        tops, masses = [], []
        for lo in range(0, q, 128):
            mask = xid == yid[:, lo : lo + 128]
            if diagonal:
                i = lax.broadcasted_iota(jnp.int32, (size, 128), 0)
                j = lax.broadcasted_iota(jnp.int32, (size, 128), 1) + lo
                mask = mask & (i != j)
            top = jnp.where(mask, scores[:, lo : lo + 128], NO_PAIR)
            mass = jnp.exp2(top * LOG2 - LOG2)
            cols = pl.ds(lo, 128)
            cacc[slot, 0, :, cols] = jnp.maximum(
                cacc[slot, 0, :, cols], jnp.max(top.reshape(size // 8, 8, 128), axis=0)
            )
            cacc[slot, 1, :, cols] += jnp.sum(mass.reshape(size // 8, 8, 128), axis=0)
            tops.append(top)
            masses.append(mass)
        if not diagonal:
            racc[xi, 0, rows, :] = jnp.maximum(
                racc[xi, 0, rows, :], functools.reduce(jnp.maximum, tops)
            )
            racc[xi, 1, rows, :] += functools.reduce(jnp.add, masses)

    def row_result(xi, start, size):
        rows = pl.ds(start, size)
        rowres[xi, 0, :, rows] = jnp.max(racc[xi, 0, rows, :].T.reshape(16, 8, size), axis=0)
        rowres[xi, 1, :, rows] = jnp.sum(racc[xi, 1, rows, :].T.reshape(16, 8, size), axis=0)

    cacc[:, 0] = jnp.full((SLOTS, 8, q), -1.0, jnp.float32)
    cacc[:, 1] = jnp.zeros((SLOTS, 8, q), jnp.float32)

    racc[:, 0] = jnp.full((3, q, 128), -1.0, jnp.float32)
    racc[:, 1] = jnp.zeros((3, q, 128), jnp.float32)
    load_x(OWN, 0)
    tile(OWN, 0, 0, q, OWN, diagonal=True)

    def arrived(slot, parts=(0, 1)):
        copies = halves(OWN, slot, 0, (sister, z))
        for part in parts:
            copies[part].wait_recv()

    across = jnp.where(low, 4 - 3 * odd, -1 - 3 * odd)
    across_from = jnp.where(low, 2 + odd, -3 + odd)
    has_across = has(across) & has(across_from)

    def go_on(slot, s, by):
        return halves(slot, slot - by, s, (d + by, z))

    go_across = go_on(REACH + across_from, 3, across)
    go_near = go_on(REACH + near, 4, sis)
    go_diag = go_on(REACH - near, 5, sis)
    has_diag = has(-near)

    for part in range(2):
        pl.when(has_far)(functools.partial(arrived, REACH + far, (part,)))
        pl.when(has_across & jnp.logical_not(ends))(go_across[part].start)
        arrived(REACH + near, (part,))
        pl.when(has_across & ends)(go_across[part].start)
        go_near[part].start()
    arrived(REACH + sis)

    order = (0, sis, near, far, near + sis, -near, -near + sis)

    def nth(i):
        k = jnp.int32(0)
        for j in range(1, SLOTS):
            k = jnp.where(i == j, order[j], k)
        return k

    def own_step(i, carry):
        k = nth(i)

        @pl.when((k > 0) & has(k))
        def _():
            tile(OWN, 0, 0, q, REACH + k)

        return carry

    lax.fori_loop(1, 4, own_step, 0)

    def diag(part):
        @pl.when(has_diag)
        def _():
            arrived(REACH - near, (part,))
            go_diag[part].start()

    def result(k):
        return remote(
            cacc.at[REACH + k],
            rbuf.at[REACH - k],
            S_RES + REACH + k,
            R_RES + REACH - k,
            (d + k, z),
        )

    def meet(slot, xi, xz, start, size, first, stop, last=False):
        def step(i, carry):
            k = nth(i)
            apart = ((k == REACH) & (xz < z - 1)) | ((k == -REACH) & (z < xz - 1))

            @pl.when(has(k) & jnp.logical_not(apart))
            def _():
                tile(slot, xi, start, size, REACH + k)

            if last:
                pl.when(has(k) & (k != 0))(lambda: result(k).start())
            return carry

        lax.fori_loop(first, stop, step, 0)

    row_a = remote(rowres.at[1], rbuf.at[ZA], S_ROW, R_RES + ZA, (d, from_a))
    row_b = remote(rowres.at[2], rbuf.at[ZB], S_ROW + 1, R_RES + ZB, (d, mate))

    diag(0)

    @pl.when(inner)
    def _():
        z_copy(2, ZB, (d, mate)).wait_recv()
        load_x(ZB, 2)
        for part in range(2):
            z_copy(part, ZB, (d, mate)).wait_recv()
        meet(ZB, 2, mate, 0, q, 0, 4)

    diag(1)
    z_copy(2, ZA, (d, from_a)).wait_recv()
    load_x(ZA, 1)
    z_copy(0, ZA, (d, from_a)).wait_recv()
    meet(ZA, 1, from_a, 0, half, 0, 4)

    pl.when(has(near + sis))(functools.partial(arrived, REACH + near + sis))
    pl.when(has(-near + sis))(functools.partial(arrived, REACH - near + sis))
    lax.fori_loop(4, SLOTS, own_step, 0)
    row_result(0, 0, q)

    @pl.when(inner)
    def _():
        meet(ZB, 2, mate, 0, q, 4, SLOTS)
        row_result(2, 0, q)
        row_b.start()

    meet(ZA, 1, from_a, 0, half, 4, SLOTS)
    row_result(1, 0, half)
    z_copy(1, ZA, (d, from_a)).wait_recv()
    meet(ZA, 1, from_a, half, half, 0, SLOTS, last=True)
    row_result(1, half, half)
    row_a.start()

    back = remote(rowres.at[3], rbuf.at[SLOTS + 2], S_ROW + 2, R_RES + SLOTS + 2, (d - 4, 3))

    @pl.when(corner_in)
    def _():
        remote(buf.at[OWN, tail], corner, S_CORNER, R_CORNER, (d - 4, 3)).wait_recv()
        first = buf[OWN, 0:16, :].astype(jnp.float32)[0:1]
        last = corner[0:16, :].astype(jnp.float32)[15:16]
        cos = jnp.sum(first * last, axis=1, keepdims=True)
        here = take_ids(OWN)[:, 0:1]
        there = corner[16:32, 0:q].astype(jnp.float32)[0:1, q - 1 : q]
        top = jnp.broadcast_to(jnp.where(here == there, cos, NO_PAIR), (8, q))
        mass = jnp.exp2(top * LOG2 - LOG2)
        mine = (lanes == 0) & (subs == 0)
        cacc[OWN, 0] = jnp.maximum(cacc[OWN, 0], jnp.where(mine, top, -1.0))
        cacc[OWN, 1] += jnp.where(mine, mass, 0.0)
        theirs = (lanes == q - 1) & (subs == 0)
        rowres[3, 0] = jnp.where(theirs, top, -1.0)
        rowres[3, 1] = jnp.where(theirs, mass, 0.0)
        back.start()

    out_ref[0] = jnp.maximum(rowres[0, 0], cacc[OWN, 0])
    out_ref[1] = rowres[0, 1] + cacc[OWN, 1]

    def add_result(slot):
        remote(rowres.at[0], rbuf.at[slot], S_ROW, R_RES + slot, (sister, z)).wait_recv()
        out_ref[0] = jnp.maximum(out_ref[0], rbuf[slot, 0])
        out_ref[1] += rbuf[slot, 1]

    pl.when(corner_out)(functools.partial(add_result, SLOTS + 2))
    for k in (-3, -2, -1, 1, 2, 3):
        pl.when(has(k))(functools.partial(add_result, REACH + k))
    add_result(ZA)
    pl.when(outer)(functools.partial(add_result, ZB))

    for part in range(3):
        z_copy(part, ZA, (d, to_a)).wait_send()
        pl.when(outer)(z_copy(part, ZB, (d, mate)).wait_send)
    for part in range(2):
        send_near[part].wait_send()
        pl.when(has_far)(send_far[part].wait_send)
        send_sis[part].wait_send()
        pl.when(has_across)(go_across[part].wait_send)
        go_near[part].wait_send()
        pl.when(has_diag)(go_diag[part].wait_send)
    pl.when(corner_out)(send_corner.wait_send)
    for k in (-3, -2, -1, 1, 2, 3):
        pl.when(has(k))(result(k).wait_send)
    row_a.wait_send()
    pl.when(inner)(row_b.wait_send)
    pl.when(corner_in)(back.wait_send)


def finish(both_ref, top_ref, mass_ref):
    top_ref[...] = jnp.max(both_ref[0], axis=0)
    mass_ref[...] = jnp.sum(both_ref[1], axis=0)


def per_device(n, embeds, cluster):
    q, width = embeds.shape
    both = pl.pallas_call(
        functools.partial(kernel, n),
        out_shape=jax.ShapeDtypeStruct((2, 8, q), jnp.float32),
        in_specs=[pl.BlockSpec(memory_space=pltpu.HBM)] * 2,
        out_specs=pl.BlockSpec(memory_space=pltpu.VMEM),
        scratch_shapes=[
            pltpu.VMEM((q, width), jnp.bfloat16),
            pltpu.VMEM((1, q), jnp.int32),
            pltpu.VMEM((SLOTS + 2, q + 16, width), jnp.bfloat16),
            pltpu.VMEM((32, width), jnp.bfloat16),
            pltpu.VMEM((3, q, 128), jnp.float32),
            pltpu.VMEM((3, 2, q, 128), jnp.float32),
            pltpu.VMEM((SLOTS, 2, 8, q), jnp.float32),
            pltpu.VMEM((4, 2, 8, q), jnp.float32),
            pltpu.VMEM((SLOTS + 3, 2, 8, q), jnp.float32),
            pltpu.SemaphoreType.DMA((S_Z + 6,)),
            pltpu.SemaphoreType.DMA((R_Z + 6,)),
            pltpu.SemaphoreType.DMA((2,)),
        ],
        compiler_params=pltpu.CompilerParams(
            collective_id=0, has_side_effects=True, vmem_limit_bytes=215 * 2**18
        ),
        name="dedup",
    )(embeds, cluster.reshape(1, q))
    return pl.pallas_call(
        finish,
        out_shape=(jax.ShapeDtypeStruct((q,), jnp.float32),) * 2,
        in_specs=[pl.BlockSpec(memory_space=pltpu.VMEM)],
        out_specs=(pl.BlockSpec(memory_space=pltpu.VMEM),) * 2,
        name="finish",
    )(both)


def solution(mesh):
    return jax.shard_map(
        functools.partial(per_device, mesh.shape["docs"]),
        mesh=mesh,
        in_specs=(P(("docs", "rep"), None), P(("docs", "rep"))),
        out_specs=(P(("docs", "rep")), P(("docs", "rep"))),
        check_vma=False,
    )
```

```python
import functools
import math

import jax
import jax.numpy as jnp
from jax import lax
from jax.experimental import pallas as pl
from jax.experimental.pallas import tpu as pltpu
from jax.sharding import PartitionSpec as P

MESH = pl.DeviceIdType.MESH
dup_scale = 8.0
LOG2 = dup_scale * math.log2(math.e)
NO_PAIR = -100.0
REACH = 3
SLOTS = 2 * REACH + 1
OWN, ZA, ZB = REACH, SLOTS, SLOTS + 1
S_CORNER = 12
S_ROW = S_CORNER + 1
S_RES = S_ROW + 3
S_Z = S_RES + SLOTS
R_CORNER = 2 * SLOTS
R_RES = R_CORNER + 1
R_Z = R_RES + SLOTS + 3


def kernel(
    n,
    e_hbm,
    c_hbm,
    out_ref,
    e_ref,
    c_ref,
    buf,
    corner,
    xids,
    racc,
    cacc,
    rowres,
    rbuf,
    ssem,
    rsem,
    lsem,
):
    q, width = e_ref.shape
    half = q // 2
    d = lax.axis_index("docs")
    z = lax.axis_index("rep")
    odd = lax.rem(d, 2)
    corner_of_four = lax.rem(d, 4)
    low = corner_of_four < 2
    sis = 1 - 2 * odd
    near = jnp.where(low, 2, -2)
    far = 6 * odd - 3
    sister = d + sis
    to_a = jnp.where(z < 2, z + 2, 3 - z)
    from_a = jnp.where(z < 2, 3 - z, z - 2)
    mate = z + 1 - 2 * lax.rem(z, 2)
    takes_b = (z == 0) | (z == 3)
    sends_b = (z == 1) | (z == 2)

    def has(k):
        return (d + k >= 0) & (d + k < n)

    corner_in = (z == 0) & has(-4)
    corner_out = (z == 3) & has(4)
    ends = (corner_of_four == 0) | (corner_of_four == 3)

    def remote(src, dst, s, r, dev):
        return pltpu.make_async_remote_copy(
            src_ref=src,
            dst_ref=dst,
            send_sem=ssem.at[s],
            recv_sem=rsem.at[r],
            device_id=dev,
            device_id_type=MESH,
        )

    barrier = pltpu.get_barrier_semaphore()

    def greet(dev):
        pl.semaphore_signal(barrier, inc=1, device_id=dev, device_id_type=MESH)

    load_e = pltpu.make_async_copy(e_hbm, e_ref, lsem.at[0])
    load_c = pltpu.make_async_copy(c_hbm, c_ref, lsem.at[1])
    load_e.start()
    load_c.start()
    total = jnp.int32(3)
    for k in (-3, -2, -1, 1, 2, 3):
        pl.when(has(k))(functools.partial(greet, (d + k, z)))
        total = total + has(k).astype(jnp.int32)
    for k in (-4, 4):
        pl.when(has(k) & ends)(functools.partial(greet, (d + k, z)))
        total = total + (has(k) & ends).astype(jnp.int32)
    greet((d, to_a))
    greet((d, from_a))
    greet((d, mate))
    pl.when(corner_in)(functools.partial(greet, (d - 4, 3)))
    pl.when(corner_out)(functools.partial(greet, (d + 4, 0)))
    total = total + corner_in.astype(jnp.int32) + corner_out.astype(jnp.int32)

    id_rows = pl.ds(q, 16)

    def z_copy(part, slot, dev):
        first = 3 * (slot - ZA)
        if part == 2:
            view = (id_rows, pl.ds(0, q))
        else:
            view = (pl.ds(part * half, half),)
        return remote(
            buf.at[(OWN,) + view],
            buf.at[(slot,) + view],
            S_Z + first + part,
            R_Z + first + part,
            dev,
        )

    def send_z(part):
        pl.when(sends_b)(z_copy(part, ZB, (d, mate)).start)
        z_copy(part, ZA, (d, to_a)).start()

    def halves(slot, to, s, dev):
        return [
            remote(buf.at[slot, view], buf.at[to, view], 2 * s + part, 2 * to + part, dev)
            for part, view in enumerate((pl.ds(0, half), pl.ds(half, half + 16)))
        ]

    send_near = halves(OWN, REACH - near, 0, (d + near, z))
    send_far = halves(OWN, REACH - far, 1, (d + far, z))
    send_sis = halves(OWN, REACH - sis, 2, (sister, z))
    has_far = has(far)
    tail = pl.ds(q - 16, 32)
    send_corner = remote(buf.at[OWN, tail], corner, S_CORNER, R_CORNER, (d + 4, 0))

    load_c.wait()
    ids = c_ref[...].astype(jnp.float32)
    buf[OWN, q : q + 16, :] = jnp.zeros((16, width), jnp.bfloat16)
    buf[OWN, q : q + 16, 0:q] = jnp.broadcast_to(ids, (16, q)).astype(jnp.bfloat16)
    load_e.wait()
    for part in range(2):
        rows = pl.ds(part * half, half)
        x = e_ref[rows, :].astype(jnp.float32)
        scale = lax.rsqrt(jnp.mean(x * x, axis=1, keepdims=True) + 1e-06)
        buf[OWN, rows, :] = (x * scale * width ** (-0.5)).astype(jnp.bfloat16)
        if part == 0:
            pl.semaphore_wait(barrier, total)
        pl.when(has_far)(send_far[part].start)
        send_near[part].start()
        send_z(part)
        send_sis[part].start()
        if part == 0:
            send_z(2)
    pl.when(corner_out)(send_corner.start)

    lanes = lax.broadcasted_iota(jnp.int32, (8, q), 1)
    subs = lax.broadcasted_iota(jnp.int32, (8, q), 0)

    def take_ids(slot):
        return buf[slot, q : q + 16, 0:q].astype(jnp.float32)[0:1]

    def load_x(slot, xi):
        xids[xi] = jnp.broadcast_to(take_ids(slot), (128, q)).T

    def tile(xslot, xi, start, size, slot, diagonal=False):
        rows = pl.ds(start, size)
        scores = lax.dot_general(
            buf[xslot, rows, :],
            buf[slot, 0:q, :],
            (((1,), (1,)), ((), ())),
            preferred_element_type=jnp.float32,
        )
        yid = take_ids(slot)
        xid = xids[xi, rows, :]
        tops, masses = [], []
        for lo in range(0, q, 128):
            mask = xid == yid[:, lo : lo + 128]
            if diagonal:
                i = lax.broadcasted_iota(jnp.int32, (size, 128), 0)
                j = lax.broadcasted_iota(jnp.int32, (size, 128), 1) + lo
                mask = mask & (i != j)
            top = jnp.where(mask, scores[:, lo : lo + 128], NO_PAIR)
            mass = jnp.exp2(top * LOG2 - LOG2)
            cols = pl.ds(lo, 128)
            cacc[slot, 0, :, cols] = jnp.maximum(
                cacc[slot, 0, :, cols], jnp.max(top.reshape(size // 8, 8, 128), axis=0)
            )
            cacc[slot, 1, :, cols] += jnp.sum(mass.reshape(size // 8, 8, 128), axis=0)
            tops.append(top)
            masses.append(mass)
        if not diagonal:
            racc[xi, 0, rows, :] = jnp.maximum(
                racc[xi, 0, rows, :], functools.reduce(jnp.maximum, tops)
            )
            racc[xi, 1, rows, :] += functools.reduce(jnp.add, masses)

    def row_result(xi, start, size):
        rows = pl.ds(start, size)
        rowres[xi, 0, :, rows] = jnp.max(racc[xi, 0, rows, :].T.reshape(16, 8, size), axis=0)
        rowres[xi, 1, :, rows] = jnp.sum(racc[xi, 1, rows, :].T.reshape(16, 8, size), axis=0)

    cacc[:, 0] = jnp.full((SLOTS, 8, q), -1.0, jnp.float32)
    cacc[:, 1] = jnp.zeros((SLOTS, 8, q), jnp.float32)

    racc[:, 0] = jnp.full((3, q, 128), -1.0, jnp.float32)
    racc[:, 1] = jnp.zeros((3, q, 128), jnp.float32)
    load_x(OWN, 0)
    tile(OWN, 0, 0, q, OWN, diagonal=True)

    def arrived(slot, parts=(0, 1)):
        copies = halves(OWN, slot, 0, (sister, z))
        for part in parts:
            copies[part].wait_recv()

    across = jnp.where(low, 4 - 3 * odd, -1 - 3 * odd)
    across_from = jnp.where(low, 2 + odd, -3 + odd)
    has_across = has(across) & has(across_from)

    def go_on(slot, s, by):
        return halves(slot, slot - by, s, (d + by, z))

    go_across = go_on(REACH + across_from, 3, across)
    go_near = go_on(REACH + near, 4, sis)
    go_diag = go_on(REACH - near, 5, sis)
    has_diag = has(-near)

    for part in range(2):
        pl.when(has_far)(functools.partial(arrived, REACH + far, (part,)))
        pl.when(has_across & jnp.logical_not(ends))(go_across[part].start)
        arrived(REACH + near, (part,))
        pl.when(has_across & ends)(go_across[part].start)
        go_near[part].start()
    arrived(REACH + sis)

    order = (0, sis, near, far, near + sis, -near, -near + sis)

    def nth(i):
        k = jnp.int32(0)
        for j in range(1, SLOTS):
            k = jnp.where(i == j, order[j], k)
        return k

    def own_step(i, carry):
        k = nth(i)

        @pl.when((k > 0) & has(k))
        def _():
            tile(OWN, 0, 0, q, REACH + k)

        return carry

    lax.fori_loop(1, 4, own_step, 0)

    def diag(part):
        @pl.when(has_diag)
        def _():
            arrived(REACH - near, (part,))
            go_diag[part].start()

    def result(k):
        return remote(
            cacc.at[REACH + k],
            rbuf.at[REACH - k],
            S_RES + REACH + k,
            R_RES + REACH - k,
            (d + k, z),
        )

    def meet(slot, xi, xz, start, size, first, stop, last=False):
        def step(i, carry):
            k = nth(i)
            apart = ((k == REACH) & (xz < z - 1)) | ((k == -REACH) & (z < xz - 1))

            @pl.when(has(k) & jnp.logical_not(apart))
            def _():
                tile(slot, xi, start, size, REACH + k)

            if last:
                pl.when(has(k) & (k != 0))(lambda: result(k).start())
            return carry

        lax.fori_loop(first, stop, step, 0)

    row_a = remote(rowres.at[1], rbuf.at[ZA], S_ROW, R_RES + ZA, (d, from_a))
    row_b = remote(rowres.at[2], rbuf.at[ZB], S_ROW + 1, R_RES + ZB, (d, mate))

    diag(0)

    @pl.when(takes_b)
    def _():
        z_copy(2, ZB, (d, mate)).wait_recv()
        load_x(ZB, 2)
        for part in range(2):
            z_copy(part, ZB, (d, mate)).wait_recv()
        meet(ZB, 2, mate, 0, q, 0, 4)

    diag(1)
    z_copy(2, ZA, (d, from_a)).wait_recv()
    load_x(ZA, 1)
    z_copy(0, ZA, (d, from_a)).wait_recv()
    meet(ZA, 1, from_a, 0, half, 0, 4)

    pl.when(has(near + sis))(functools.partial(arrived, REACH + near + sis))
    pl.when(has(-near + sis))(functools.partial(arrived, REACH - near + sis))
    lax.fori_loop(4, SLOTS, own_step, 0)
    row_result(0, 0, q)

    @pl.when(takes_b)
    def _():
        meet(ZB, 2, mate, 0, q, 4, SLOTS)
        row_result(2, 0, q)
        row_b.start()

    meet(ZA, 1, from_a, 0, half, 4, SLOTS)
    row_result(1, 0, half)
    z_copy(1, ZA, (d, from_a)).wait_recv()
    meet(ZA, 1, from_a, half, half, 0, SLOTS, last=True)
    row_result(1, half, half)
    row_a.start()

    back = remote(rowres.at[3], rbuf.at[SLOTS + 2], S_ROW + 2, R_RES + SLOTS + 2, (d - 4, 3))

    @pl.when(corner_in)
    def _():
        remote(buf.at[OWN, tail], corner, S_CORNER, R_CORNER, (d - 4, 3)).wait_recv()
        first = buf[OWN, 0:16, :].astype(jnp.float32)[0:1]
        last = corner[0:16, :].astype(jnp.float32)[15:16]
        cos = jnp.sum(first * last, axis=1, keepdims=True)
        here = take_ids(OWN)[:, 0:1]
        there = corner[16:32, 0:q].astype(jnp.float32)[0:1, q - 1 : q]
        top = jnp.broadcast_to(jnp.where(here == there, cos, NO_PAIR), (8, q))
        mass = jnp.exp2(top * LOG2 - LOG2)
        mine = (lanes == 0) & (subs == 0)
        cacc[OWN, 0] = jnp.maximum(cacc[OWN, 0], jnp.where(mine, top, -1.0))
        cacc[OWN, 1] += jnp.where(mine, mass, 0.0)
        theirs = (lanes == q - 1) & (subs == 0)
        rowres[3, 0] = jnp.where(theirs, top, -1.0)
        rowres[3, 1] = jnp.where(theirs, mass, 0.0)
        back.start()

    out_ref[0] = jnp.maximum(rowres[0, 0], cacc[OWN, 0])
    out_ref[1] = rowres[0, 1] + cacc[OWN, 1]

    def add_result(slot):
        remote(rowres.at[0], rbuf.at[slot], S_ROW, R_RES + slot, (sister, z)).wait_recv()
        out_ref[0] = jnp.maximum(out_ref[0], rbuf[slot, 0])
        out_ref[1] += rbuf[slot, 1]

    pl.when(corner_out)(functools.partial(add_result, SLOTS + 2))
    for k in (-3, -2, -1, 1, 2, 3):
        pl.when(has(k))(functools.partial(add_result, REACH + k))
    add_result(ZA)
    pl.when(sends_b)(functools.partial(add_result, ZB))

    for part in range(3):
        z_copy(part, ZA, (d, to_a)).wait_send()
        pl.when(sends_b)(z_copy(part, ZB, (d, mate)).wait_send)
    for part in range(2):
        send_near[part].wait_send()
        pl.when(has_far)(send_far[part].wait_send)
        send_sis[part].wait_send()
        pl.when(has_across)(go_across[part].wait_send)
        go_near[part].wait_send()
        pl.when(has_diag)(go_diag[part].wait_send)
    pl.when(corner_out)(send_corner.wait_send)
    for k in (-3, -2, -1, 1, 2, 3):
        pl.when(has(k))(result(k).wait_send)
    row_a.wait_send()
    pl.when(takes_b)(row_b.wait_send)
    pl.when(corner_in)(back.wait_send)


def finish(both_ref, top_ref, mass_ref):
    top_ref[...] = jnp.max(both_ref[0], axis=0)
    mass_ref[...] = jnp.sum(both_ref[1], axis=0)


def per_device(n, embeds, cluster):
    q, width = embeds.shape
    both = pl.pallas_call(
        functools.partial(kernel, n),
        out_shape=jax.ShapeDtypeStruct((2, 8, q), jnp.float32),
        in_specs=[pl.BlockSpec(memory_space=pltpu.HBM)] * 2,
        out_specs=pl.BlockSpec(memory_space=pltpu.VMEM),
        scratch_shapes=[
            pltpu.VMEM((q, width), jnp.bfloat16),
            pltpu.VMEM((1, q), jnp.int32),
            pltpu.VMEM((SLOTS + 2, q + 16, width), jnp.bfloat16),
            pltpu.VMEM((32, width), jnp.bfloat16),
            pltpu.VMEM((3, q, 128), jnp.float32),
            pltpu.VMEM((3, 2, q, 128), jnp.float32),
            pltpu.VMEM((SLOTS, 2, 8, q), jnp.float32),
            pltpu.VMEM((4, 2, 8, q), jnp.float32),
            pltpu.VMEM((SLOTS + 3, 2, 8, q), jnp.float32),
            pltpu.SemaphoreType.DMA((S_Z + 6,)),
            pltpu.SemaphoreType.DMA((R_Z + 6,)),
            pltpu.SemaphoreType.DMA((2,)),
        ],
        compiler_params=pltpu.CompilerParams(
            collective_id=0, has_side_effects=True, vmem_limit_bytes=63 * 2**20
        ),
        name="dedup",
    )(embeds, cluster.reshape(1, q))
    return pl.pallas_call(
        finish,
        out_shape=(jax.ShapeDtypeStruct((q,), jnp.float32),) * 2,
        in_specs=[pl.BlockSpec(memory_space=pltpu.VMEM)],
        out_specs=(pl.BlockSpec(memory_space=pltpu.VMEM),) * 2,
        name="finish",
    )(both)


def solution(mesh):
    return jax.shard_map(
        functools.partial(per_device, mesh.shape["docs"]),
        mesh=mesh,
        in_specs=(P(("docs", "rep"), None), P(("docs", "rep"))),
        out_specs=(P(("docs", "rep")), P(("docs", "rep"))),
        check_vma=False,
    )
```

```python
import functools
import math

import jax
import jax.numpy as jnp
from jax import lax
from jax.experimental import pallas as pl
from jax.experimental.pallas import tpu as pltpu
from jax.sharding import PartitionSpec as P

MESH = pl.DeviceIdType.MESH
dup_scale = 8.0
LOG2 = dup_scale * math.log2(math.e)
NO_PAIR = -100.0
REACH = 3
SLOTS = 2 * REACH + 1
OWN, ZA, ZB = REACH, SLOTS, SLOTS + 1
S_CORNER = 12
S_ROW = S_CORNER + 1
S_RES = S_ROW + 3
S_Z = S_RES + SLOTS
R_CORNER = 2 * SLOTS
R_RES = R_CORNER + 1
R_Z = R_RES + SLOTS + 3


def kernel(
    n,
    e_hbm,
    c_hbm,
    out_ref,
    e_ref,
    c_ref,
    buf,
    corner,
    xids,
    racc,
    cacc,
    rowres,
    rbuf,
    ssem,
    rsem,
    lsem,
):
    q, width = e_ref.shape
    half = q // 2
    d = lax.axis_index("docs")
    z = lax.axis_index("rep")
    odd = lax.rem(d, 2)
    corner_of_four = lax.rem(d, 4)
    low = corner_of_four < 2
    sis = 1 - 2 * odd
    near = jnp.where(low, 2, -2)
    far = 6 * odd - 3
    sister = d + sis
    to_a = jnp.where(z < 2, z + 2, 3 - z)
    from_a = jnp.where(z < 2, 3 - z, z - 2)
    mate = z + 1 - 2 * lax.rem(z, 2)
    inner = (z == 1) | (z == 2)
    outer = (z == 0) | (z == 3)

    def has(k):
        return (d + k >= 0) & (d + k < n)

    corner_in = (z == 0) & has(-4)
    corner_out = (z == 3) & has(4)
    ends = (corner_of_four == 0) | (corner_of_four == 3)

    def remote(src, dst, s, r, dev):
        return pltpu.make_async_remote_copy(
            src_ref=src,
            dst_ref=dst,
            send_sem=ssem.at[s],
            recv_sem=rsem.at[r],
            device_id=dev,
            device_id_type=MESH,
        )

    barrier = pltpu.get_barrier_semaphore()

    def greet(dev):
        pl.semaphore_signal(barrier, inc=1, device_id=dev, device_id_type=MESH)

    load_e = pltpu.make_async_copy(e_hbm, e_ref, lsem.at[0])
    load_c = pltpu.make_async_copy(c_hbm, c_ref, lsem.at[1])
    load_e.start()
    load_c.start()
    total = jnp.int32(3)
    for k in (-3, -2, -1, 1, 2, 3):
        pl.when(has(k))(functools.partial(greet, (d + k, z)))
        total = total + has(k).astype(jnp.int32)
    for k in (-4, 4):
        pl.when(has(k) & ends)(functools.partial(greet, (d + k, z)))
        total = total + (has(k) & ends).astype(jnp.int32)
    greet((d, to_a))
    greet((d, from_a))
    greet((d, mate))
    pl.when(corner_in)(functools.partial(greet, (d - 4, 3)))
    pl.when(corner_out)(functools.partial(greet, (d + 4, 0)))
    total = total + corner_in.astype(jnp.int32) + corner_out.astype(jnp.int32)

    id_rows = pl.ds(q, 16)

    def z_copy(part, slot, dev):
        first = 3 * (slot - ZA)
        if part == 2:
            view = (id_rows, pl.ds(0, q))
        else:
            view = (pl.ds(part * half, half),)
        return remote(
            buf.at[(OWN,) + view],
            buf.at[(slot,) + view],
            S_Z + first + part,
            R_Z + first + part,
            dev,
        )

    def send_z(part):
        pl.when(outer)(z_copy(part, ZB, (d, mate)).start)
        z_copy(part, ZA, (d, to_a)).start()

    def halves(slot, to, s, dev):
        return [
            remote(buf.at[slot, view], buf.at[to, view], 2 * s + part, 2 * to + part, dev)
            for part, view in enumerate((pl.ds(0, half), pl.ds(half, half + 16)))
        ]

    send_near = halves(OWN, REACH - near, 0, (d + near, z))
    send_far = halves(OWN, REACH - far, 1, (d + far, z))
    send_sis = halves(OWN, REACH - sis, 2, (sister, z))
    has_far = has(far)
    tail = pl.ds(q - 16, 32)
    send_corner = remote(buf.at[OWN, tail], corner, S_CORNER, R_CORNER, (d + 4, 0))

    load_c.wait()
    ids = c_ref[...].astype(jnp.float32)
    buf[OWN, q : q + 16, :] = jnp.zeros((16, width), jnp.bfloat16)
    buf[OWN, q : q + 16, 0:q] = jnp.broadcast_to(ids, (16, q)).astype(jnp.bfloat16)
    load_e.wait()
    for part in range(2):
        rows = pl.ds(part * half, half)
        x = e_ref[rows, :].astype(jnp.float32)
        scale = lax.rsqrt(jnp.mean(x * x, axis=1, keepdims=True) + 1e-06)
        buf[OWN, rows, :] = (x * scale * width ** (-0.5)).astype(jnp.bfloat16)
        if part == 0:
            pl.semaphore_wait(barrier, total)
        send_near[part].start()
        pl.when(has_far)(send_far[part].start)
        send_z(part)
        send_sis[part].start()
        if part == 0:
            send_z(2)
    pl.when(corner_out)(send_corner.start)

    lanes = lax.broadcasted_iota(jnp.int32, (8, q), 1)
    subs = lax.broadcasted_iota(jnp.int32, (8, q), 0)

    def take_ids(slot):
        return buf[slot, q : q + 16, 0:q].astype(jnp.float32)[0:1]

    def load_x(slot, xi):
        xids[xi] = jnp.broadcast_to(take_ids(slot), (128, q)).T

    def tile(xslot, xi, start, size, slot, diagonal=False):
        rows = pl.ds(start, size)
        scores = lax.dot_general(
            buf[xslot, rows, :],
            buf[slot, 0:q, :],
            (((1,), (1,)), ((), ())),
            preferred_element_type=jnp.float32,
        )
        yid = take_ids(slot)
        xid = xids[xi, rows, :]
        tops, masses = [], []
        for lo in range(0, q, 128):
            mask = xid == yid[:, lo : lo + 128]
            if diagonal:
                i = lax.broadcasted_iota(jnp.int32, (size, 128), 0)
                j = lax.broadcasted_iota(jnp.int32, (size, 128), 1) + lo
                mask = mask & (i != j)
            top = jnp.where(mask, scores[:, lo : lo + 128], NO_PAIR)
            mass = jnp.exp2(top * LOG2 - LOG2)
            cols = pl.ds(lo, 128)
            cacc[slot, 0, :, cols] = jnp.maximum(
                cacc[slot, 0, :, cols], jnp.max(top.reshape(size // 8, 8, 128), axis=0)
            )
            cacc[slot, 1, :, cols] += jnp.sum(mass.reshape(size // 8, 8, 128), axis=0)
            tops.append(top)
            masses.append(mass)
        if not diagonal:
            racc[xi, 0, rows, :] = jnp.maximum(
                racc[xi, 0, rows, :], functools.reduce(jnp.maximum, tops)
            )
            racc[xi, 1, rows, :] += functools.reduce(jnp.add, masses)

    def row_result(xi, start, size):
        rows = pl.ds(start, size)
        rowres[xi, 0, :, rows] = jnp.max(racc[xi, 0, rows, :].T.reshape(16, 8, size), axis=0)
        rowres[xi, 1, :, rows] = jnp.sum(racc[xi, 1, rows, :].T.reshape(16, 8, size), axis=0)

    cacc[:, 0] = jnp.full((SLOTS, 8, q), -1.0, jnp.float32)
    cacc[:, 1] = jnp.zeros((SLOTS, 8, q), jnp.float32)

    racc[:, 0] = jnp.full((3, q, 128), -1.0, jnp.float32)
    racc[:, 1] = jnp.zeros((3, q, 128), jnp.float32)
    load_x(OWN, 0)
    tile(OWN, 0, 0, q, OWN, diagonal=True)

    def arrived(slot, parts=(0, 1)):
        copies = halves(OWN, slot, 0, (sister, z))
        for part in parts:
            copies[part].wait_recv()

    across = jnp.where(low, 4 - 3 * odd, -1 - 3 * odd)
    across_from = jnp.where(low, 2 + odd, -3 + odd)
    has_across = has(across) & has(across_from)

    def go_on(slot, s, by):
        return halves(slot, slot - by, s, (d + by, z))

    go_across = go_on(REACH + across_from, 3, across)
    go_near = go_on(REACH + near, 4, sis)
    go_diag = go_on(REACH - near, 5, sis)
    has_diag = has(-near)

    for part in range(2):
        pl.when(has_far)(functools.partial(arrived, REACH + far, (part,)))
        pl.when(has_across & jnp.logical_not(ends))(go_across[part].start)
        arrived(REACH + near, (part,))
        pl.when(has_across & ends)(go_across[part].start)
        go_near[part].start()
    arrived(REACH + sis)

    order = (0, sis, near, far, near + sis, -near, -near + sis)

    def nth(i):
        k = jnp.int32(0)
        for j in range(1, SLOTS):
            k = jnp.where(i == j, order[j], k)
        return k

    def own_step(i, carry):
        k = nth(i)

        @pl.when((k > 0) & has(k))
        def _():
            tile(OWN, 0, 0, q, REACH + k)

        return carry

    lax.fori_loop(1, 4, own_step, 0)

    def diag(part):
        @pl.when(has_diag)
        def _():
            arrived(REACH - near, (part,))
            go_diag[part].start()

    def result(k):
        return remote(
            cacc.at[REACH + k],
            rbuf.at[REACH - k],
            S_RES + REACH + k,
            R_RES + REACH - k,
            (d + k, z),
        )

    def meet(slot, xi, xz, start, size, first, stop, last=False):
        def step(i, carry):
            k = nth(i)
            apart = ((k == REACH) & (xz < z - 1)) | ((k == -REACH) & (z < xz - 1))

            @pl.when(has(k) & jnp.logical_not(apart))
            def _():
                tile(slot, xi, start, size, REACH + k)

            if last:
                pl.when(has(k) & (k != 0))(lambda: result(k).start())
            return carry

        lax.fori_loop(first, stop, step, 0)

    row_a = remote(rowres.at[1], rbuf.at[ZA], S_ROW, R_RES + ZA, (d, from_a))
    row_b = remote(rowres.at[2], rbuf.at[ZB], S_ROW + 1, R_RES + ZB, (d, mate))

    diag(0)

    @pl.when(inner)
    def _():
        z_copy(2, ZB, (d, mate)).wait_recv()
        load_x(ZB, 2)
        for part in range(2):
            z_copy(part, ZB, (d, mate)).wait_recv()
        meet(ZB, 2, mate, 0, q, 0, 4)

    diag(1)
    z_copy(2, ZA, (d, from_a)).wait_recv()
    load_x(ZA, 1)
    z_copy(0, ZA, (d, from_a)).wait_recv()
    meet(ZA, 1, from_a, 0, half, 0, 4)

    pl.when(has(near + sis))(functools.partial(arrived, REACH + near + sis))
    pl.when(has(-near + sis))(functools.partial(arrived, REACH - near + sis))
    lax.fori_loop(4, SLOTS, own_step, 0)
    row_result(0, 0, q)

    @pl.when(inner)
    def _():
        meet(ZB, 2, mate, 0, q, 4, SLOTS)
        row_result(2, 0, q)
        row_b.start()

    meet(ZA, 1, from_a, 0, half, 4, SLOTS)
    row_result(1, 0, half)
    z_copy(1, ZA, (d, from_a)).wait_recv()
    meet(ZA, 1, from_a, half, half, 0, SLOTS, last=True)
    row_result(1, half, half)
    row_a.start()

    back = remote(rowres.at[3], rbuf.at[SLOTS + 2], S_ROW + 2, R_RES + SLOTS + 2, (d - 4, 3))

    @pl.when(corner_in)
    def _():
        remote(buf.at[OWN, tail], corner, S_CORNER, R_CORNER, (d - 4, 3)).wait_recv()
        first = buf[OWN, 0:16, :].astype(jnp.float32)[0:1]
        last = corner[0:16, :].astype(jnp.float32)[15:16]
        cos = jnp.sum(first * last, axis=1, keepdims=True)
        here = take_ids(OWN)[:, 0:1]
        there = corner[16:32, 0:q].astype(jnp.float32)[0:1, q - 1 : q]
        top = jnp.broadcast_to(jnp.where(here == there, cos, NO_PAIR), (8, q))
        mass = jnp.exp2(top * LOG2 - LOG2)
        mine = (lanes == 0) & (subs == 0)
        cacc[OWN, 0] = jnp.maximum(cacc[OWN, 0], jnp.where(mine, top, -1.0))
        cacc[OWN, 1] += jnp.where(mine, mass, 0.0)
        theirs = (lanes == q - 1) & (subs == 0)
        rowres[3, 0] = jnp.where(theirs, top, -1.0)
        rowres[3, 1] = jnp.where(theirs, mass, 0.0)
        back.start()

    out_ref[0] = jnp.maximum(rowres[0, 0], cacc[OWN, 0])
    out_ref[1] = rowres[0, 1] + cacc[OWN, 1]

    def add_result(slot):
        remote(rowres.at[0], rbuf.at[slot], S_ROW, R_RES + slot, (sister, z)).wait_recv()
        out_ref[0] = jnp.maximum(out_ref[0], rbuf[slot, 0])
        out_ref[1] += rbuf[slot, 1]

    pl.when(corner_out)(functools.partial(add_result, SLOTS + 2))
    for k in (-3, -2, -1, 1, 2, 3):
        pl.when(has(k))(functools.partial(add_result, REACH + k))
    add_result(ZA)
    pl.when(outer)(functools.partial(add_result, ZB))

    for part in range(3):
        z_copy(part, ZA, (d, to_a)).wait_send()
        pl.when(outer)(z_copy(part, ZB, (d, mate)).wait_send)
    for part in range(2):
        send_near[part].wait_send()
        pl.when(has_far)(send_far[part].wait_send)
        send_sis[part].wait_send()
        pl.when(has_across)(go_across[part].wait_send)
        go_near[part].wait_send()
        pl.when(has_diag)(go_diag[part].wait_send)
    pl.when(corner_out)(send_corner.wait_send)
    for k in (-3, -2, -1, 1, 2, 3):
        pl.when(has(k))(result(k).wait_send)
    row_a.wait_send()
    pl.when(inner)(row_b.wait_send)
    pl.when(corner_in)(back.wait_send)


def finish(both_ref, top_ref, mass_ref):
    top_ref[...] = jnp.max(both_ref[0], axis=0)
    mass_ref[...] = jnp.sum(both_ref[1], axis=0)


def per_device(n, embeds, cluster):
    q, width = embeds.shape
    both = pl.pallas_call(
        functools.partial(kernel, n),
        out_shape=jax.ShapeDtypeStruct((2, 8, q), jnp.float32),
        in_specs=[pl.BlockSpec(memory_space=pltpu.HBM)] * 2,
        out_specs=pl.BlockSpec(memory_space=pltpu.VMEM),
        scratch_shapes=[
            pltpu.VMEM((q, width), jnp.bfloat16),
            pltpu.VMEM((1, q), jnp.int32),
            pltpu.VMEM((SLOTS + 2, q + 16, width), jnp.bfloat16),
            pltpu.VMEM((32, width), jnp.bfloat16),
            pltpu.VMEM((3, q, 128), jnp.float32),
            pltpu.VMEM((3, 2, q, 128), jnp.float32),
            pltpu.VMEM((SLOTS, 2, 8, q), jnp.float32),
            pltpu.VMEM((4, 2, 8, q), jnp.float32),
            pltpu.VMEM((SLOTS + 3, 2, 8, q), jnp.float32),
            pltpu.SemaphoreType.DMA((S_Z + 6,)),
            pltpu.SemaphoreType.DMA((R_Z + 6,)),
            pltpu.SemaphoreType.DMA((2,)),
        ],
        compiler_params=pltpu.CompilerParams(
            collective_id=0, has_side_effects=True, vmem_limit_bytes=63 * 2**20
        ),
        name="dedup",
    )(embeds, cluster.reshape(1, q))
    return pl.pallas_call(
        finish,
        out_shape=(jax.ShapeDtypeStruct((q,), jnp.float32),) * 2,
        in_specs=[pl.BlockSpec(memory_space=pltpu.VMEM)],
        out_specs=(pl.BlockSpec(memory_space=pltpu.VMEM),) * 2,
        name="finish",
    )(both)


def solution(mesh):
    return jax.shard_map(
        functools.partial(per_device, mesh.shape["docs"]),
        mesh=mesh,
        in_specs=(P(("docs", "rep"), None), P(("docs", "rep"))),
        out_specs=(P(("docs", "rep")), P(("docs", "rep"))),
        check_vma=False,
    )
```
